256 devices in a mesh: section: 8 (over z), dp: 32 (over x, y, core).
Axes of the slice: x: 4, y: 4, z: 8, core: 2. Of those that a mesh axis runs over, the one named last changes fastest.
Arguments:
- patches: bfloat16 [96, 240, 1536], P('dp'), may hold values from -6 to 6
- kept: int32 [96, 120], P('dp'), may hold values from 0 to 239, as said below
- segment_ids: int32 [96, 240], P('dp'), may hold values from 0 to 3, never falling along the last dimension, each value on 1 to 120 neighbouring positions
- pos_embed: bfloat16 [240, 1536], replicated, may hold values from -6 to 6
- mask_token: bfloat16 [1536], replicated, may hold values from -6 to 6
- w_query: bfloat16 [8, 1536, 1536], P('section', 'dp'), may hold values from -0.15625 to 0.15625
- w_key: bfloat16 [8, 1536, 1536], P('section', 'dp'), may hold values from -0.15625 to 0.15625
- w_value: bfloat16 [8, 1536, 1536], P('section', 'dp'), may hold values from -0.15625 to 0.15625
- w_out: bfloat16 [8, 1536, 1536], P('section', 'dp'), may hold values from -0.15625 to 0.15625
Outputs:
- section_out: bfloat16 [8, 96, 240, 1536], P('section', 'dp')
The draws below stay inside these ranges and needn't reach their ends.
Inputs may be any that keep to these rules, and one draw needn't show every extreme that they name: `kept`: each row holds 120 distinct patch positions.
All inputs are finite; a program needn't handle non-finite values.
Results may differ from the reference program's by a relative error of at most 0.017.
Values may be sent and summed in bfloat16 or wider, within the bound.
No kernel may reach another device: no remote copies, remote signals or barrier semaphores. Data moves between devices by JAX's collectives and lax.ppermute only.
A program may use at most 128 MiB of HBM per device.

```python
import math
import jax
import jax.numpy as jnp
import numpy as np
from jax import lax

D = 1536
HEADS = 12
HEAD_DIM = 128
HD = 1536
P_SIZE = 240
K = 120
SEGS = 4
SECTIONS = 8
ENC = 4
SAMPLES = 96


def draw_kept(key, part):
    key = jax.random.fold_in(key, 11)
    sample_keys = jax.random.split(key, SAMPLES)

    def choose(sample_key):
        return jax.random.permutation(sample_key, P_SIZE)[:K]
    return jax.vmap(choose)(sample_keys).astype(jnp.int32)


def block_scale(rng, shape, cuts, least, largest):
    level, own = 1.0, jax.random.fold_in(rng, 6)
    for axis_at, parts in cuts:
        draws = jnp.exp(jax.random.uniform(jax.random.fold_in(own, axis_at), (parts,), jnp.float32, least / len(cuts), largest / len(cuts)))
        level = level * jnp.repeat(draws, shape[axis_at] // parts).reshape([-1 if axis == axis_at else 1 for axis in range(len(shape))])
    return level


def profile(count, total, bound, lean):
    loads = [(1 << 20) // math.isqrt(grade ** lean) + 1 for grade in range(2, count + 1)]
    spare, holding = total - bound - (count - 1), [1] * (count - 1)
    while spare > 0:
        movable = [i for i in range(count - 1) if holding[i] < bound]
        mass, left = sum([loads[i] for i in movable]), spare
        for i in movable:
            more = min(bound - holding[i], max(1, left * loads[i] // mass), spare)
            holding[i] = holding[i] + more
            spare = spare - more
    return np.array([bound] + holding)


def ragged(key, count, total, limit, slope):
    if count == 2:
        one = jax.random.randint(key, (), max(1, total - limit), min(limit, total - 1) + 1)
        return jnp.stack([one, total - one])
    lengths = jnp.asarray(profile(count, total, limit, slope), jnp.int32)
    twos = (count - 1) // 2
    giver, receiver = lengths[1:1 + 2 * twos:2], lengths[2:2 + 2 * twos:2]
    room = jnp.minimum(giver - 1, limit - receiver)
    passed = jax.random.randint(jax.random.fold_in(key, 1), (twos,), 0, 1 << 20) % (room + 1)
    lengths = lengths.at[1:1 + 2 * twos:2].set(giver - passed).at[2:2 + 2 * twos:2].set(receiver + passed)
    return lengths[jax.random.permutation(jax.random.fold_in(key, 2), count)]


def gaussian(own_key, extent, width, most, shards=(), dtype=jnp.bfloat16):
    gain = block_scale(own_key, extent, shards, -0.22, 0.18) if shards else 1.0
    array = jax.random.normal(own_key, extent, jnp.float32) * width * gain
    return jnp.minimum(jnp.maximum(array, -most), most).astype(dtype)


def setup_inputs(seed: int = 0) -> dict:
    key_of = jax.random.split(jax.random.key(seed), 10)
    patches = gaussian(key_of[0], (SAMPLES, P_SIZE, D), 1.0, 6.0, ((0, 32),))
    kept = draw_kept(jax.random.fold_in(key_of[9], 71), 0)
    segment_ids = jax.vmap(lambda own: jnp.searchsorted(jnp.cumsum(ragged(own, SEGS, P_SIZE, P_SIZE // 2, 2)), jnp.arange(P_SIZE), side="right"))(jax.random.split(key_of[2], SAMPLES)).reshape((SAMPLES, P_SIZE)).astype(jnp.int32)
    pos_embed = gaussian(key_of[3], (P_SIZE, D), 1.0, 6.0)
    mask_token = gaussian(key_of[4], (D,), 1.0, 6.0)
    w_query = gaussian(key_of[5], (SECTIONS, D, HD), D ** -0.5, 0.15625, ((0, 8), (1, 32)))
    w_key = gaussian(key_of[6], (SECTIONS, D, HD), D ** -0.5, 0.15625, ((0, 8), (1, 32)))
    w_value = gaussian(key_of[7], (SECTIONS, D, HD), D ** -0.5, 0.15625, ((0, 8), (1, 32)))
    w_out = gaussian(key_of[8], (SECTIONS, HD, D), HD ** -0.5, 0.15625, ((0, 8), (1, 32)))
    return {"patches": patches, "kept": kept, "segment_ids": segment_ids, "pos_embed": pos_embed, "mask_token": mask_token, "w_query": w_query, "w_key": w_key, "w_value": w_value, "w_out": w_out}


def rms_rows(vector):
    return vector * lax.rsqrt(lax.optimization_barrier(jnp.mean(vector * vector, axis=-1, keepdims=True)) + 1e-06)

def attend_layer(hidden, segment, w_query, w_key, w_value, w_out):
    row_count = hidden.shape[0]
    normed = rms_rows(hidden.astype(jnp.float32)).astype(jnp.bfloat16)

    def project(weight):
        return jnp.dot(normed, weight, preferred_element_type=jnp.float32).reshape(row_count, HEADS, HEAD_DIM)
    queries = rms_rows(project(w_query)).astype(jnp.bfloat16)
    keys_all = rms_rows(project(w_key)).astype(jnp.bfloat16)
    values = project(w_value).astype(jnp.bfloat16)
    scores = jnp.einsum('qhd,khd->hqk', queries.astype(jnp.float32), keys_all.astype(jnp.float32)) / jnp.sqrt(jnp.float32(HEAD_DIM))
    same_seg = segment[:, None] == segment[None, :]
    expo = jnp.where(same_seg[None], jnp.exp(scores), jnp.float32(0.0))
    attn_probs = (expo / lax.optimization_barrier(jnp.sum(expo, axis=-1, keepdims=True))).astype(jnp.bfloat16)
    mixed_heads = jnp.einsum('hqk,khd->qhd', attn_probs.astype(jnp.float32), values.astype(jnp.float32))
    mixed_heads = mixed_heads.astype(jnp.bfloat16).reshape(row_count, HD)
    return (hidden.astype(jnp.float32) + jnp.dot(mixed_heads, w_out, preferred_element_type=jnp.float32)).astype(jnp.bfloat16)

def reference(patches, kept, segment_ids, pos_embed, mask_token, w_query, w_key, w_value, w_out):
    filler_base = mask_token.astype(jnp.float32)[None, :] + pos_embed.astype(jnp.float32)

    def one_sample(item):
        sample, positions, segment = item
        table = (jnp.arange(P_SIZE)[:, None] == positions[None, :]).astype(jnp.bfloat16)
        flag = lax.optimization_barrier(jnp.sum(table.astype(jnp.float32), axis=1))
        hidden = jnp.dot(table.T, sample, preferred_element_type=jnp.float32).astype(jnp.bfloat16)
        seg_kept = jnp.take(segment, positions)
        outputs = []
        for layer in range(SECTIONS):
            if layer < ENC:
                hidden = attend_layer(hidden, seg_kept, w_query[layer], w_key[layer], w_value[layer], w_out[layer])
                outputs.append(jnp.dot(table, hidden, preferred_element_type=jnp.float32).astype(jnp.bfloat16))
            else:
                if layer == ENC:
                    hidden = (outputs[-1].astype(jnp.float32) + (1.0 - flag)[:, None] * filler_base).astype(jnp.bfloat16)
                hidden = attend_layer(hidden, segment, w_query[layer], w_key[layer], w_value[layer], w_out[layer])
                outputs.append(hidden)
        return jnp.stack(outputs)
    result = lax.map(one_sample, (patches, kept, segment_ids))
    return jnp.transpose(result, (1, 0, 2, 3))
```

```python
import functools
import jax
import jax.numpy as jnp
from jax import lax
from jax.experimental import pallas as pl
from jax.experimental.pallas import tpu as pltpu
from jax.sharding import Mesh, PartitionSpec as P

D = 1536
HEADS = 12
HEAD_DIM = 128
SECTIONS = 8
ENC = 4
MICRO = 3
ROWS = 240
KEPT = 120
KROWS = 128
CHIPS = 16
PART = 48
EPS = 1e-06
WSHAPE = (CHIPS, 2, PART, D)
VM = pl.BlockSpec(memory_space=pltpu.VMEM)
SM = pl.BlockSpec(memory_space=pltpu.SMEM)
HB = pl.BlockSpec(memory_space=pl.ANY)


def in_vmem(array):
    return pltpu.with_memory_space_constraint(array, pltpu.VMEM)


def load_kernel(count, info, own, other, *rest):
    outs, sems = rest[:count], rest[count]
    core = info[1]
    copies = []
    for i in range(count):
        rows = pl.ds(i * PART, PART)
        copies.append(pltpu.make_async_copy(own.at[:, rows], outs[i].at[:, core], sems.at[2 * i]))
        copies.append(
            pltpu.make_async_copy(other.at[:, rows], outs[i].at[:, 1 - core], sems.at[2 * i + 1])
        )
    for copy in copies:
        copy.start()
    for copy in copies:
        copy.wait()


def load_weights(info, own, other, count):
    return pl.pallas_call(
        functools.partial(load_kernel, count),
        out_shape=[pltpu.VMEM(WSHAPE, jnp.bfloat16)] * count,
        in_specs=[SM, HB, HB],
        out_specs=[VM] * count,
        scratch_shapes=[pltpu.SemaphoreType.DMA((2 * count,))],
        compiler_params=pltpu.CompilerParams(vmem_limit_bytes=4 << 20),
        cost_estimate=pl.CostEstimate(
            flops=0, bytes_accessed=4 * count * D * D, transcendentals=0
        ),
        name="load_weights",
    )(info, own, other)


def rms(x):
    return x * lax.rsqrt(jnp.mean(x * x, axis=-1, keepdims=True) + EPS)


def dot(a, b):
    return jnp.dot(a, b, preferred_element_type=jnp.float32)


def table_of(kept_row, rows):
    pos = lax.broadcasted_iota(jnp.int32, (rows, KROWS), 0)
    return pos == kept_row


def layer(hid, nrm, ho, wq, wk, wv, wo, seg_col, seg_row, out):
    nrm[...] = rms(hid[...].astype(jnp.float32)).astype(jnp.bfloat16)
    same = seg_col == seg_row
    scale = HEAD_DIM**-0.5
    for pair in range(HEADS // 2):
        cols = pl.ds(pair * 256, 256)

        def project(weight):
            return dot(nrm[...], weight[:, :, :, cols].reshape(D, 256))

        q2, k2, v2 = project(wq), project(wk), project(wv).astype(jnp.bfloat16)
        for half in range(2):
            lanes = slice(half * HEAD_DIM, (half + 1) * HEAD_DIM)
            q = rms(q2[:, lanes]).astype(jnp.bfloat16)
            k = rms(k2[:, lanes]).astype(jnp.bfloat16)
            s = lax.dot_general(
                q, k, (((1,), (1,)), ((), ())), preferred_element_type=jnp.float32
            )
            e = jnp.where(same, jnp.exp(s * scale), 0.0)
            total = jnp.sum(e, axis=-1, keepdims=True)
            o = dot(e.astype(jnp.bfloat16), v2[:, lanes]) / total
            ho[:, pl.ds(pair * 256 + half * HEAD_DIM, HEAD_DIM)] = o.astype(jnp.bfloat16)
    for part in range(D // 256):
        cols = pl.ds(part * 256, 256)
        y = dot(ho[...], wo[:, :, :, cols].reshape(D, 256))
        out[:, cols] = (hid[:, cols].astype(jnp.float32) + y).astype(jnp.bfloat16)


def micro_of(info, tick, first, last):
    section = info[0]
    micro = tick - section
    active = (micro >= 0) & (micro < MICRO) & (section >= first) & (section < last)
    return section, jnp.clip(micro, 0, MICRO - 1), active


def enc_kernel(tick, info, start, recv, seg_c, seg_r, wq, wk, wv, wo, out, hid, nrm, ho):
    section, micro, active = micro_of(info, tick, 0, ENC)

    @pl.when(active)
    def _():
        @pl.when(section == 0)
        def _():
            hid[...] = start[micro]

        @pl.when(section != 0)
        def _():
            hid[...] = recv[...]

        layer(hid, nrm, ho, wq, wk, wv, wo, seg_c[micro], seg_r[micro], out)


def dec_kernel(
    tick, info, recv_e, recv_d, kept, pos, mask, seg_c, seg_r, wq, wk, wv, wo, buf, out, done,
    hid, nrm, ho, sem
):
    section, micro, active = micro_of(info, tick, ENC, SECTIONS)

    @pl.when(active)
    def _():
        @pl.when(section == ENC)
        def _():
            table = table_of(kept[micro], ROWS).astype(jnp.float32)
            flag = jnp.sum(table, axis=1, keepdims=True)
            rows = dot(table.astype(jnp.bfloat16), recv_e[...])
            base = mask[...].astype(jnp.float32) + pos[...].astype(jnp.float32)
            hid[...] = (rows + (1.0 - flag) * base).astype(jnp.bfloat16)

        @pl.when(section != ENC)
        def _():
            hid[...] = recv_d[...]

        layer(hid, nrm, ho, wq, wk, wv, wo, seg_c[micro], seg_r[micro], out)
        copy = pltpu.make_async_copy(out, done.at[micro], sem)
        copy.start()
        copy.wait()


def put_kernel(tick, info, res, kept, buf, done, wide, sem):
    section, micro, active = micro_of(info, tick, 0, ENC)

    @pl.when(active)
    def _():
        table = table_of(kept[micro], ROWS).astype(jnp.bfloat16)
        wide[...] = dot(table, res[...]).astype(jnp.bfloat16)
        copy = pltpu.make_async_copy(wide, done.at[micro], sem)
        copy.start()
        copy.wait()


def start_kernel(patches, kept, out):
    for micro in range(MICRO):
        table = table_of(kept[micro], ROWS).astype(jnp.bfloat16)
        out[micro] = lax.dot_general(
            table, patches[micro], (((0,), (0,)), ((), ())), preferred_element_type=jnp.float32
        ).astype(jnp.bfloat16)


def cost(rows):
    return pl.CostEstimate(
        flops=2 * 4 * rows * D * D, bytes_accessed=8 * D * D, transcendentals=HEADS * rows * rows
    )


def params():
    return pltpu.CompilerParams(vmem_limit_bytes=12 << 20)


def bf16(*shape):
    return jax.ShapeDtypeStruct(shape, jnp.bfloat16)


def on_device(patches, kept, segment_ids, pos_embed, mask_token, w_query, w_key, w_value, w_out):
    section = lax.axis_index("section")
    core = lax.axis_index("core")
    info = jnp.stack([section, core]).astype(jnp.int32)
    swap = [(0, 1), (1, 0)]
    qkv = jnp.concatenate([w_query[0], w_key[0], w_value[0]], axis=0)
    own_qkv = lax.all_gather(qkv, ("x", "y"), axis=0, tiled=False)
    own_out = lax.all_gather(w_out[0], ("x", "y"), axis=0, tiled=False)
    other_qkv = lax.ppermute(own_qkv, "core", swap)
    other_out = lax.ppermute(own_out, "core", swap)

    padded = jnp.pad(kept, ((0, 0), (0, KROWS - KEPT)), constant_values=-1)
    hit = padded[:, :, None] == jnp.arange(ROWS, dtype=jnp.int32)[None, None, :]
    kept_seg = jnp.sum(jnp.where(hit, segment_ids[:, None, :], 0), axis=2)
    kept_seg = jnp.where(padded < 0, -1, kept_seg).astype(jnp.int32)
    kept_row = padded[:, None, :]
    enc_c, enc_r = kept_seg[:, :, None], kept_seg[:, None, :]
    dec_c, dec_r = segment_ids[:, :, None], segment_ids[:, None, :]
    mask_row = mask_token[None, :]

    start = pl.pallas_call(
        start_kernel, out_shape=bf16(MICRO, KROWS, D), in_specs=[VM, VM], out_specs=VM,
        compiler_params=params(), name="start_rows",
    )(patches, kept_row)

    wq, wk, wv = load_weights(info, own_qkv, other_qkv, 3)
    own_out, other_out, wq = lax.optimization_barrier((own_out, other_out, wq))
    (wo,) = load_weights(info, own_out, other_out, 1)
    weights = [in_vmem(w) for w in (wq, wk, wv, wo)]

    buf = jnp.zeros((MICRO, ROWS, D), jnp.bfloat16)
    recv_e = jnp.zeros((KROWS, D), jnp.bfloat16)
    recv_d = jnp.zeros((ROWS, D), jnp.bfloat16)
    for tick in range(MICRO + SECTIONS - 1):
        active = range(max(0, tick - MICRO + 1), min(SECTIONS - 1, tick) + 1)
        next_e, next_d, res_e = recv_e, recv_d, None
        if active[0] < ENC:
            res_e = pl.pallas_call(
                functools.partial(enc_kernel, tick), out_shape=bf16(KROWS, D),
                in_specs=[SM] + [VM] * 8, out_specs=VM,
                scratch_shapes=[pltpu.VMEM((KROWS, D), jnp.bfloat16)] * 3,
                compiler_params=params(), cost_estimate=cost(KROWS), name="encoder_layer",
            )(info, start, recv_e, enc_c, enc_r, *weights)
            next_e = lax.ppermute(res_e, "section", [(s, s + 1) for s in active if s < ENC])
        if active[-1] >= ENC:
            res_d, buf = pl.pallas_call(
                functools.partial(dec_kernel, tick),
                out_shape=[bf16(ROWS, D), bf16(MICRO, ROWS, D)],
                in_specs=[SM] + [VM] * 11 + [HB], out_specs=[VM, HB],
                scratch_shapes=[pltpu.VMEM((ROWS, D), jnp.bfloat16)] * 3
                + [pltpu.SemaphoreType.DMA],
                input_output_aliases={12: 1},
                compiler_params=params(), cost_estimate=cost(ROWS), name="decoder_layer",
            )(info, recv_e, recv_d, kept_row, pos_embed, mask_row, dec_c, dec_r, *weights, buf)
            pairs = [(s, s + 1) for s in active if ENC <= s < SECTIONS - 1]
            if pairs:
                next_d = lax.ppermute(res_d, "section", pairs)
        if res_e is not None:
            buf = pl.pallas_call(
                functools.partial(put_kernel, tick), out_shape=bf16(MICRO, ROWS, D),
                in_specs=[SM, VM, VM, HB], out_specs=HB,
                scratch_shapes=[pltpu.VMEM((ROWS, D), jnp.bfloat16), pltpu.SemaphoreType.DMA],
                input_output_aliases={3: 0},
                compiler_params=params(),
                cost_estimate=pl.CostEstimate(
                    flops=2 * ROWS * KROWS * D, bytes_accessed=8 * ROWS * D, transcendentals=0
                ),
                name="put_rows",
            )(info, res_e, kept_row, buf)
        recv_e, recv_d = next_e, next_d
    return buf[None]


def solution(mesh):
    grid = Mesh(mesh.devices.reshape(SECTIONS, 4, 4, 2), ("section", "x", "y", "core"))
    dp = ("x", "y", "core")
    in_specs = (
        P(dp, None, None),
        P(dp, None),
        P(dp, None),
        P(),
        P(),
        P("section", dp, None),
        P("section", dp, None),
        P("section", dp, None),
        P("section", dp, None),
    )
    out_specs = P("section", dp, None, None)
    return jax.shard_map(
        on_device, mesh=grid, in_specs=in_specs, out_specs=out_specs, check_vma=False
    )
```

```python
import functools
import jax
import jax.numpy as jnp
from jax import lax
from jax.experimental import pallas as pl
from jax.experimental.pallas import tpu as pltpu
from jax.sharding import Mesh, PartitionSpec as P

D = 1536
HEADS = 12
HEAD_DIM = 128
SECTIONS = 8
ENC = 4
MICRO = 3
ROWS = 240
KEPT = 120
KROWS = 128
PART = 48
EPS = 1e-06
LOG2E = 1.4426950408889634
UNROLL = 5
UNROLL_OUT = 6
WSHAPE = (4, 4, 2, PART, D)
VM = pl.BlockSpec(memory_space=pltpu.VMEM)
SM = pl.BlockSpec(memory_space=pltpu.SMEM)
HB = pl.BlockSpec(memory_space=pl.ANY)


def in_vmem(array):
    return pltpu.with_memory_space_constraint(array, pltpu.VMEM)


def move_kernel(count, plan, info, *rest):
    ins, outs, sems = rest[:count], rest[count:-1], rest[-1]
    copies = []
    for i, (source, at, target, to) in enumerate(plan):
        src = ins[source] if at is None else ins[source].at[at]
        copies.append(pltpu.make_async_copy(src, outs[target].at[to(info)], sems.at[i]))
    for copy in copies:
        copy.start()
    for copy in copies:
        copy.wait()


def move(info, ins, shapes, plan, name):
    results = pl.pallas_call(
        functools.partial(move_kernel, len(ins), plan),
        out_shape=[bf16(*shape) for shape in shapes],
        in_specs=[SM] + [HB] * len(ins),
        out_specs=[HB] * len(shapes),
        scratch_shapes=[pltpu.SemaphoreType.DMA((len(plan),))],
        compiler_params=pltpu.CompilerParams(vmem_limit_bytes=2 << 20),
        cost_estimate=pl.CostEstimate(flops=0, bytes_accessed=3 << 20, transcendentals=0),
        name=name,
    )(info, *ins)
    return list(results)


def fixed(*index):
    return lambda info: index


def load_kernel(pieces, keeps, info, *rest):
    count = len(pieces)
    ins, outs, sems = rest[:count], rest[-5:-1], rest[-1]
    core = info[1]
    copies = []
    for ref, (group, shift, half, swapped) in zip(ins, pieces):
        side = 1 - core if swapped else core
        far = (info[3 - group] + shift) & 3
        for w in range(2):
            if half is not None and half != w:
                continue
            src = ref if half is not None else ref.at[w]
            at = (slice(None), far, side) if group == 0 else (far, slice(None), side)
            copies.append(
                pltpu.make_async_copy(src, outs[group + 2 * w].at[at], sems.at[len(copies)])
            )
    for copy in copies:
        copy.start()
    for copy in copies:
        copy.wait()


def load(info, arrays, pieces, kept=()):
    arrays = [pltpu.with_memory_space_constraint(p, pltpu.HBM) for p in arrays]
    kept = [in_vmem(w) for w in kept]
    return pl.pallas_call(
        functools.partial(load_kernel, pieces, len(kept)),
        out_shape=[pltpu.VMEM(WSHAPE, jnp.bfloat16)] * 4,
        in_specs=[SM] + [HB] * len(arrays) + [VM] * len(kept),
        out_specs=[VM] * 4,
        input_output_aliases={1 + len(arrays) + i: i for i in range(len(kept))},
        scratch_shapes=[pltpu.SemaphoreType.DMA((2 * len(pieces),))],
        compiler_params=pltpu.CompilerParams(vmem_limit_bytes=2 << 20),
        cost_estimate=pl.CostEstimate(flops=0, bytes_accessed=8 * D * D, transcendentals=0),
        name="load_weights",
    )(info, *arrays, *kept)


def shifted(block, axis, by):
    return lax.ppermute(block, axis, [(i, (i + by) % 4) for i in range(4)])


def swapped(block):
    return lax.ppermute(block, "core", [(0, 1), (1, 0)])


def gathered(w_query, w_key, w_value, w_out, info):
    axes = (("x", "y"), ("y", "x"))
    ws = (w_query, w_key, w_value, w_out)
    pairs = move(
        info, ws, [(2, PART, D)] * 2,
        [(i, None, i % 2, fixed(i // 2)) for i in range(4)], "pair_weights",
    )
    near = [[shifted(pairs[g], axes[g][0], by) for by in (1, -1)] for g in range(2)]
    flat = [near[g][i] for g in range(2) for i in range(2)]
    ahead = move(
        info, flat, [(1, PART, D)] * 4, [(i, i % 2, i, fixed(0)) for i in range(4)], "halves"
    )
    across = [
        shifted(ahead[2 * g + i], axes[g][0], (1, -1)[i]) for g in range(2) for i in range(2)
    ]

    def place(group, w, shift):
        return lambda info: (w, (info[2 + group] + shift) & 3)

    plan = []
    for g in range(2):
        for w in range(2):
            plan.append((g, w, g, place(g, w, 0)))
            plan.append((2 + 2 * g, w, g, place(g, w, 3)))
            plan.append((3 + 2 * g, w, g, place(g, w, 1)))
            plan.append((6 + 2 * g + w, 0, g, place(g, w, 2)))
    bands = move(info, pairs + flat + across, [(2, 4, PART, D)] * 2, plan, "bands")
    next_to = [[shifted(bands[g], axes[g][1], by) for by in (1, -1)] for g in range(2)]
    flat = [next_to[g][i] for g in range(2) for i in range(2)]
    ahead = move(
        info, flat, [(1, 4, PART, D)] * 4, [(i, i % 2, i, fixed(0)) for i in range(4)], "band_halves"
    )
    last = [
        shifted(ahead[2 * g + i][0], axes[g][1], (1, -1)[i]) for g in range(2) for i in range(2)
    ]
    first = bands + flat
    tags = [(0, 0, None), (1, 0, None), (0, 3, None), (0, 1, None), (1, 3, None), (1, 1, None)]
    ends = [(g, 2, w) for g in range(2) for w in range(2)]
    weights = load(
        info, first + [swapped(p) for p in first],
        [t + (False,) for t in tags] + [t + (True,) for t in tags],
    )
    return load(
        info, last + [swapped(p) for p in last],
        [t + (False,) for t in ends] + [t + (True,) for t in ends], weights,
    )


def rms(x):
    return x * lax.rsqrt(jnp.mean(x * x, axis=-1, keepdims=True) + EPS)


def dot(a, b):
    return jnp.dot(a, b, preferred_element_type=jnp.float32)


def table_of(kept_row, rows):
    pos = lax.broadcasted_iota(jnp.int32, (rows, KROWS), 0)
    return pos == kept_row


def layer(hid, nrm, ho, wq, wk, wv, wo, seg_col, seg_row, out):
    rows = hid.shape[0]
    nrm[...] = rms(hid[...].astype(jnp.float32)).astype(jnp.bfloat16)
    bias = jnp.where(seg_col == seg_row, 0.0, -1e30)
    scale = HEAD_DIM**-0.5 * LOG2E
    ones = jnp.ones((rows, HEAD_DIM), jnp.bfloat16)

    def heads_of(pair):
        cols = pl.ds(pl.multiple_of(pair * 256, 256), 256)

        def project(weight):
            return dot(nrm[...], weight[:, :, :, :, cols].reshape(D, 256))

        q2, k2, v2 = project(wq), project(wk), project(wv).astype(jnp.bfloat16)
        parts = []
        for half in range(2):
            lanes = slice(half * HEAD_DIM, (half + 1) * HEAD_DIM)
            parts.append(rms(q2[:, lanes]).astype(jnp.bfloat16))
            parts.append(rms(k2[:, lanes]).astype(jnp.bfloat16))
            parts.append(v2[:, lanes])
        return tuple(parts)

    def attend(pair, parts):
        cols = pl.ds(pl.multiple_of(pair * 256, 256), 256)
        mixed = []
        for half in range(2):
            q, k, v = parts[3 * half : 3 * half + 3]
            s = lax.dot_general(
                q, k, (((1,), (1,)), ((), ())), preferred_element_type=jnp.float32
            )
            e = jnp.exp2(s * scale + bias).astype(jnp.bfloat16)
            o = dot(e, jnp.concatenate([v, ones], axis=1))
            mixed.append((o[:, :HEAD_DIM] / o[:, HEAD_DIM:]).astype(jnp.bfloat16))
        ho[:, cols] = jnp.concatenate(mixed, axis=1)

    def step(pair, parts):
        later = heads_of(pair + 1)
        attend(pair, parts)
        return later

    last = lax.fori_loop(0, HEADS // 2 - 1, step, heads_of(0), unroll=UNROLL)
    attend(HEADS // 2 - 1, last)

    @pl.loop(0, D // 256, unroll=UNROLL_OUT)
    def _(part):
        cols = pl.ds(pl.multiple_of(part * 256, 256), 256)
        y = dot(ho[...], wo[:, :, :, :, cols].reshape(D, 256))
        out[:, cols] = (hid[:, cols].astype(jnp.float32) + y).astype(jnp.bfloat16)


def micro_of(info, tick, first, last):
    section = info[0]
    micro = tick - section
    active = (micro >= 0) & (micro < MICRO) & (section >= first) & (section < last)
    return section, jnp.clip(micro, 0, MICRO - 1), active


def enc_kernel(
    tick, only, info, start, recv_0, recv_1, seg_c, seg_r, wq, wk, wv, wo, after, out, hid, nrm, ho
):
    section, micro, active = micro_of(info, tick, 0, ENC)
    core = info[1]
    if only is not None:
        active = active & (core == only)

    @pl.when(active)
    def _():
        @pl.when(section == 0)
        def _():
            hid[...] = start[micro]

        @pl.when((section != 0) & (core == 0))
        def _():
            hid[...] = recv_0[...]

        @pl.when((section != 0) & (core == 1))
        def _():
            hid[...] = recv_1[...]

        layer(hid, nrm, ho, wq, wk, wv, wo, seg_c[micro], seg_r[micro], out)


def dec_kernel(
    tick, info, recv_e, recv_d, kept, pos, mask, seg_c, seg_r, wq, wk, wv, wo, buf, out, done,
    hid, nrm, ho, sem
):
    section, micro, active = micro_of(info, tick, ENC, SECTIONS)

    @pl.when(active)
    def _():
        @pl.when(section == ENC)
        def _():
            table = table_of(kept[micro], ROWS).astype(jnp.float32)
            flag = jnp.sum(table, axis=1, keepdims=True)
            rows = dot(table.astype(jnp.bfloat16), recv_e[...])
            base = mask[...].astype(jnp.float32) + pos[...].astype(jnp.float32)
            hid[...] = (rows + (1.0 - flag) * base).astype(jnp.bfloat16)

        @pl.when(section != ENC)
        def _():
            hid[...] = recv_d[...]

        layer(hid, nrm, ho, wq, wk, wv, wo, seg_c[micro], seg_r[micro], out)
        copy = pltpu.make_async_copy(out, done.at[micro], sem)
        copy.start()
        copy.wait()


def put_kernel(tick, info, res_0, res_1, kept, buf, done, wide, sem):
    section, micro, active = micro_of(info, tick, 0, ENC)

    @pl.when(active)
    def _():
        table = table_of(kept[micro], ROWS).astype(jnp.bfloat16)
        own = jnp.where(info[1] == 0, res_0[...].astype(jnp.float32), res_1[...].astype(jnp.float32))
        wide[...] = dot(table, own.astype(jnp.bfloat16)).astype(jnp.bfloat16)
        copy = pltpu.make_async_copy(wide, done.at[micro], sem)
        copy.start()
        copy.wait()


def start_kernel(patches, kept, out):
    for micro in range(MICRO):
        table = table_of(kept[micro], ROWS).astype(jnp.bfloat16)
        out[micro] = lax.dot_general(
            table, patches[micro], (((0,), (0,)), ((), ())), preferred_element_type=jnp.float32
        ).astype(jnp.bfloat16)


def cost(rows):
    return pl.CostEstimate(
        flops=2 * 4 * rows * D * D, bytes_accessed=8 * D * D, transcendentals=HEADS * rows * rows
    )


def params():
    return pltpu.CompilerParams(vmem_limit_bytes=12 << 20)


def bf16(*shape):
    return jax.ShapeDtypeStruct(shape, jnp.bfloat16)


def on_device(patches, kept, segment_ids, pos_embed, mask_token, w_query, w_key, w_value, w_out):
    section = lax.axis_index("section")
    core = lax.axis_index("core")
    at_x, at_y = lax.axis_index("x"), lax.axis_index("y")
    info = jnp.stack([section, core, at_x, at_y]).astype(jnp.int32)
    padded = jnp.pad(kept, ((0, 0), (0, KROWS - KEPT)), constant_values=-1)
    hit = padded[:, :, None] == jnp.arange(ROWS, dtype=jnp.int32)[None, None, :]
    kept_seg = jnp.sum(jnp.where(hit, segment_ids[:, None, :], 0), axis=2)
    kept_seg = jnp.where(padded < 0, -1, kept_seg).astype(jnp.int32)
    kept_row = padded[:, None, :]
    enc_c, enc_r = kept_seg[:, :, None], kept_seg[:, None, :]
    dec_c, dec_r = segment_ids[:, :, None], segment_ids[:, None, :]
    mask_row = mask_token[None, :]

    start = pl.pallas_call(
        start_kernel, out_shape=bf16(MICRO, KROWS, D), in_specs=[VM, VM], out_specs=VM,
        compiler_params=params(), name="start_rows",
    )(patches, kept_row)

    weights = gathered(w_query[0], w_key[0], w_value[0], w_out[0], info)
    weights = [in_vmem(w) for w in weights]

    buf = jnp.zeros((MICRO, ROWS, D), jnp.bfloat16)
    recv_e = jnp.zeros((KROWS, D), jnp.bfloat16)
    recv_d = jnp.zeros((ROWS, D), jnp.bfloat16)
    def encode(tick, recv, only=None, after=info):
        return pl.pallas_call(
            functools.partial(enc_kernel, tick, only), out_shape=bf16(KROWS, D),
            in_specs=[SM] + [VM] * 9 + [HB], out_specs=VM,
            scratch_shapes=[pltpu.VMEM((KROWS, D), jnp.bfloat16)] * 3,
            compiler_params=params(), cost_estimate=cost(KROWS), name="encoder_layer",
        )(info, start, *recv, enc_c, enc_r, *weights, after)

    recv_e = (recv_e, recv_e)
    for tick in range(MICRO + SECTIONS - 1):
        active = range(max(0, tick - MICRO + 1), min(SECTIONS - 1, tick) + 1)
        next_e, next_d, res_e = recv_e, recv_d, None
        pairs = [(s, s + 1) for s in active if s < ENC]
        if tick == 0:
            both = ("section", "core")
            res_0 = encode(tick, recv_e, only=0)
            sent_0 = lax.ppermute(res_0, both, [(0, 2)])
            token = lax.ppermute(res_0[:16, :128], both, [(0, 1)])
            res_1 = encode(tick, recv_e, only=1, after=token)
            sent_1 = lax.ppermute(res_1, both, [(1, 3)])
            res_e, next_e = (res_0, res_1), (sent_0, sent_1)
        elif active[0] < ENC:
            res = encode(tick, recv_e)
            sent = lax.ppermute(res, "section", pairs)
            res_e, next_e = (res, res), (sent, sent)
        if active[-1] >= ENC:
            res_d, buf = pl.pallas_call(
                functools.partial(dec_kernel, tick),
                out_shape=[bf16(ROWS, D), bf16(MICRO, ROWS, D)],
                in_specs=[SM] + [VM] * 11 + [HB], out_specs=[VM, HB],
                scratch_shapes=[pltpu.VMEM((ROWS, D), jnp.bfloat16)] * 3
                + [pltpu.SemaphoreType.DMA],
                input_output_aliases={12: 1},
                compiler_params=params(), cost_estimate=cost(ROWS), name="decoder_layer",
            )(info, recv_e[0], recv_d, kept_row, pos_embed, mask_row, dec_c, dec_r, *weights, buf)
            pairs = [(s, s + 1) for s in active if ENC <= s < SECTIONS - 1]
            if pairs:
                next_d = lax.ppermute(res_d, "section", pairs)
        if res_e is not None:
            buf = pl.pallas_call(
                functools.partial(put_kernel, tick), out_shape=bf16(MICRO, ROWS, D),
                in_specs=[SM, VM, VM, VM, HB], out_specs=HB,
                scratch_shapes=[pltpu.VMEM((ROWS, D), jnp.bfloat16), pltpu.SemaphoreType.DMA],
                input_output_aliases={4: 0},
                compiler_params=params(),
                cost_estimate=pl.CostEstimate(
                    flops=2 * ROWS * KROWS * D, bytes_accessed=8 * ROWS * D, transcendentals=0
                ),
                name="put_rows",
            )(info, *res_e, kept_row, buf)
        recv_e, recv_d = next_e, next_d
    return buf[None]


def solution(mesh):
    grid = Mesh(mesh.devices.reshape(SECTIONS, 4, 4, 2), ("section", "x", "y", "core"))
    dp = ("x", "y", "core")
    in_specs = (
        P(dp, None, None),
        P(dp, None),
        P(dp, None),
        P(),
        P(),
        P("section", dp, None),
        P("section", dp, None),
        P("section", dp, None),
        P("section", dp, None),
    )
    out_specs = P("section", dp, None, None)
    return jax.shard_map(
        on_device, mesh=grid, in_specs=in_specs, out_specs=out_specs, check_vma=False
    )
```

```python
import functools
import jax
import jax.numpy as jnp
from jax import lax
from jax.experimental import pallas as pl
from jax.experimental.pallas import tpu as pltpu
from jax.sharding import Mesh, PartitionSpec as P

D = 1536
HEADS = 12
HEAD_DIM = 128
SECTIONS = 8
ENC = 4
MICRO = 3
ROWS = 240
KEPT = 120
KROWS = 128
PART = 48
EPS = 1e-06
LOG2E = 1.4426950408889634
UNROLL = 5
UNROLL_OUT = 6
WSHAPE = (4, 4, 2, PART, D)
VM = pl.BlockSpec(memory_space=pltpu.VMEM)
SM = pl.BlockSpec(memory_space=pltpu.SMEM)
HB = pl.BlockSpec(memory_space=pl.ANY)


def in_vmem(array):
    return pltpu.with_memory_space_constraint(array, pltpu.VMEM)


def move_kernel(count, plan, info, *rest):
    ins, outs = rest[:count], rest[count:]
    for source, at, target, to in plan:
        outs[target][to(info)] = ins[source][...] if at is None else ins[source][at]


def move(info, ins, shapes, plan, name, after=()):
    results = pl.pallas_call(
        lambda info, *refs: move_kernel(len(ins), plan, info, *refs[: len(ins)], *refs[len(ins) + len(after) :]),
        out_shape=[bf16(*shape) for shape in shapes],
        in_specs=[SM] + [VM] * len(ins) + [HB] * len(after),
        out_specs=[VM] * len(shapes),
        compiler_params=pltpu.CompilerParams(vmem_limit_bytes=6 << 20),
        cost_estimate=pl.CostEstimate(flops=0, bytes_accessed=3 << 20, transcendentals=0),
        name=name,
    )(info, *ins, *after)
    return list(results)


def pair_kernel(info, wq, wk, wv, wo, out_0, out_1, sems):
    copies = [
        pltpu.make_async_copy(w, (out_0, out_1)[i % 2].at[i // 2], sems.at[i])
        for i, w in enumerate((wq, wk, wv, wo))
    ]
    for copy in copies:
        copy.start()
    for copy in copies:
        copy.wait()


def pair_up(info, ws):
    ws = [pltpu.with_memory_space_constraint(w, pltpu.HBM) for w in ws]
    return list(
        pl.pallas_call(
            pair_kernel,
            out_shape=[bf16(2, PART, D)] * 2,
            in_specs=[SM] + [HB] * 4,
            out_specs=[HB] * 2,
            scratch_shapes=[pltpu.SemaphoreType.DMA((4,))],
            compiler_params=pltpu.CompilerParams(vmem_limit_bytes=2 << 20),
            name="pair_weights",
        )(info, *ws)
    )


def pack_kernel(count, *rest):
    out, sems = rest[-2:]
    copies = [pltpu.make_async_copy(rest[i], out.at[i], sems.at[i]) for i in range(count)]
    for copy in copies:
        copy.start()
    for copy in copies:
        copy.wait()


def pack(ins, after):
    return pl.pallas_call(
        functools.partial(pack_kernel, len(ins)),
        out_shape=bf16(len(ins), *ins[0].shape),
        in_specs=[HB] * (len(ins) + len(after)),
        out_specs=HB,
        scratch_shapes=[pltpu.SemaphoreType.DMA((len(ins),))],
        compiler_params=pltpu.CompilerParams(vmem_limit_bytes=2 << 20),
        cost_estimate=pl.CostEstimate(flops=0, bytes_accessed=14 << 20, transcendentals=0),
        name="pack",
    )(*ins, *after)


def fixed(*index):
    return lambda info: index


def load_kernel(pieces, first, info, *rest):
    count = len(pieces)
    ins, outs, sems = rest[:count], rest[-5:-1], rest[-1]
    core = info[1]
    todo = []
    for ref, piece in zip(ins, pieces):
        if isinstance(piece, list):
            todo += [(ref.at[i], tag + (True,)) for i, tag in enumerate(piece)]
        else:
            todo.append((ref, piece))
    copies = []
    for ref, (group, shift, half, swapped) in todo:
        side = 1 - core if swapped else core
        far = (info[3 - group] + shift) & 3
        for w in range(2):
            if half is not None and half != w:
                continue
            src = ref if half is not None else ref.at[w]
            at = (slice(None), far, side) if group == 0 else (far, slice(None), side)
            copies.append(
                pltpu.make_async_copy(src, outs[group + 2 * w].at[at], sems.at[len(copies)])
            )

    @pl.when((info[0] >= first) & (info[0] < first + ENC))
    def _():
        for copy in copies:
            copy.start()
        for copy in copies:
            copy.wait()


def load(info, arrays, pieces, first, kept=(), after=()):
    arrays = [pltpu.with_memory_space_constraint(p, pltpu.HBM) for p in arrays]
    kept = [in_vmem(w) for w in kept]
    return pl.pallas_call(
        functools.partial(load_kernel, pieces, first),
        out_shape=[pltpu.VMEM(WSHAPE, jnp.bfloat16)] * 4,
        in_specs=[SM] + [HB] * (len(arrays) + len(after)) + [VM] * len(kept),
        out_specs=[VM] * 4,
        input_output_aliases={1 + len(arrays) + len(after) + i: i for i in range(len(kept))},
        scratch_shapes=[pltpu.SemaphoreType.DMA((32,))],
        compiler_params=pltpu.CompilerParams(vmem_limit_bytes=2 << 20),
        cost_estimate=pl.CostEstimate(flops=0, bytes_accessed=8 * D * D, transcendentals=0),
        name="load_weights",
    )(info, *arrays, *after, *kept)


def shifted(block, axis, by):
    return lax.ppermute(block, axis, [(i, (i + by) % 4) for i in range(4)])


def swapped(block):
    return lax.ppermute(block, "core", [(0, 1), (1, 0)])


def gathered(w_query, w_key, w_value, w_out, info):
    axes = (("x", "y"), ("y", "x"))
    ws = (w_query, w_key, w_value, w_out)
    pairs = pair_up(info, ws)
    near = [[shifted(pairs[g], axes[g][0], by) for by in (1, -1)] for g in range(2)]
    flat = [near[g][i] for g in range(2) for i in range(2)]
    ahead = move(
        info, flat, [(1, PART, D)] * 4, [(i, i % 2, i, fixed(0)) for i in range(4)], "halves"
    )
    across = [
        shifted(ahead[2 * g + i], axes[g][0], (1, -1)[i]) for g in range(2) for i in range(2)
    ]

    def place(group, w, shift):
        return lambda info: (w, (info[2 + group] + shift) & 3)

    plan = []
    for g in range(2):
        for w in range(2):
            plan.append((g, w, g, place(g, w, 0)))
            plan.append((2 + 2 * g, w, g, place(g, w, 3)))
            plan.append((3 + 2 * g, w, g, place(g, w, 1)))
            plan.append((6 + 2 * g + w, 0, g, place(g, w, 2)))
    bands = move(info, pairs + flat + across, [(2, 4, PART, D)] * 2, plan, "bands")
    next_to = [[shifted(bands[g], axes[g][1], by) for by in (1, -1)] for g in range(2)]
    flat = [next_to[g][i] for g in range(2) for i in range(2)]
    ahead = move(
        info, flat, [(1, 4, PART, D)] * 4, [(i, i % 2, i, fixed(0)) for i in range(4)],
        "band_halves",
    )
    last = [
        shifted(ahead[2 * g + i][0], axes[g][1], (1, -1)[i]) for g in range(2) for i in range(2)
    ]
    packed = swapped(pack(bands + flat, ahead))
    tags = [(0, 0, None), (1, 0, None), (0, 3, None), (0, 1, None), (1, 3, None), (1, 1, None)]
    ends = [(g, 2, w) for g in range(2) for w in range(2)]
    early, early_tags = bands + flat + [packed], [t + (False,) for t in tags] + [tags]
    late = last + [swapped(p) for p in last]
    late_tags = [t + (False,) for t in ends] + [t + (True,) for t in ends]
    weights = load(info, early, early_tags, 0)
    weights = load(info, late, late_tags, 0, weights)

    def decoder_weights(after):
        return load(info, early + late, early_tags + late_tags, ENC, after=after)

    return weights, decoder_weights


def rms(x):
    return x * lax.rsqrt(jnp.mean(x * x, axis=-1, keepdims=True) + EPS)


def dot(a, b):
    return jnp.dot(a, b, preferred_element_type=jnp.float32)


def table_of(kept_row, rows):
    pos = lax.broadcasted_iota(jnp.int32, (rows, KROWS), 0)
    return pos == kept_row


def layer(hid, nrm, ho, wq, wk, wv, wo, seg_col, seg_row, out):
    rows = hid.shape[0]
    nrm[...] = rms(hid[...].astype(jnp.float32)).astype(jnp.bfloat16)
    bias = jnp.where(seg_col == seg_row, 0.0, -1e30)
    scale = HEAD_DIM**-0.5 * LOG2E
    ones = jnp.ones((rows, HEAD_DIM), jnp.bfloat16)

    def heads_of(pair):
        cols = pl.ds(pl.multiple_of(pair * 256, 256), 256)

        def project(weight):
            return dot(nrm[...], weight[:, :, :, :, cols].reshape(D, 256))

        q2, k2, v2 = project(wq), project(wk), project(wv).astype(jnp.bfloat16)
        parts = []
        for half in range(2):
            lanes = slice(half * HEAD_DIM, (half + 1) * HEAD_DIM)
            parts.append(rms(q2[:, lanes]).astype(jnp.bfloat16))
            parts.append(rms(k2[:, lanes]).astype(jnp.bfloat16))
            parts.append(v2[:, lanes])
        return tuple(parts)

    def attend(pair, parts):
        cols = pl.ds(pl.multiple_of(pair * 256, 256), 256)
        mixed = []
        for half in range(2):
            q, k, v = parts[3 * half : 3 * half + 3]
            s = lax.dot_general(
                q, k, (((1,), (1,)), ((), ())), preferred_element_type=jnp.float32
            )
            e = jnp.exp2(s * scale + bias).astype(jnp.bfloat16)
            o = dot(e, jnp.concatenate([v, ones], axis=1))
            mixed.append((o[:, :HEAD_DIM] / o[:, HEAD_DIM:]).astype(jnp.bfloat16))
        ho[:, cols] = jnp.concatenate(mixed, axis=1)

    def step(pair, parts):
        later = heads_of(pair + 1)
        attend(pair, parts)
        return later

    last = lax.fori_loop(0, HEADS // 2 - 1, step, heads_of(0), unroll=UNROLL)
    attend(HEADS // 2 - 1, last)

    @pl.loop(0, D // 256, unroll=UNROLL_OUT)
    def _(part):
        cols = pl.ds(pl.multiple_of(part * 256, 256), 256)
        y = dot(ho[...], wo[:, :, :, :, cols].reshape(D, 256))
        out[:, cols] = (hid[:, cols].astype(jnp.float32) + y).astype(jnp.bfloat16)


def micro_of(info, tick, first, last):
    section = info[0]
    micro = tick - section
    active = (micro >= 0) & (micro < MICRO) & (section >= first) & (section < last)
    return section, jnp.clip(micro, 0, MICRO - 1), active


def enc_kernel(
    tick, only, info, start, recv_0, recv_1, seg_c, seg_r, wq, wk, wv, wo, after, out, hid, nrm, ho
):
    section, micro, active = micro_of(info, tick, 0, ENC)
    core = info[1]
    if only is not None:
        active = active & (core == only)

    @pl.when(active)
    def _():
        @pl.when(section == 0)
        def _():
            hid[...] = start[micro]

        @pl.when((section != 0) & (core == 0))
        def _():
            hid[...] = recv_0[...]

        @pl.when((section != 0) & (core == 1))
        def _():
            hid[...] = recv_1[...]

        layer(hid, nrm, ho, wq, wk, wv, wo, seg_c[micro], seg_r[micro], out)


def dec_kernel(
    tick, info, recv_e, recv_0, recv_1, kept, pos, mask, seg_c, seg_r, wq, wk, wv, wo, out,
    hid, nrm, ho
):
    section, micro, active = micro_of(info, tick, ENC, SECTIONS)

    @pl.when(active)
    def _():
        @pl.when(section == ENC)
        def _():
            table = table_of(kept[micro], ROWS).astype(jnp.float32)
            flag = jnp.sum(table, axis=1, keepdims=True)
            rows = dot(table.astype(jnp.bfloat16), recv_e[...])
            base = mask[...].astype(jnp.float32) + pos[...].astype(jnp.float32)
            hid[...] = (rows + (1.0 - flag) * base).astype(jnp.bfloat16)

        @pl.when((section != ENC) & (info[1] == 0))
        def _():
            hid[...] = recv_0[...]

        @pl.when((section != ENC) & (info[1] == 1))
        def _():
            hid[...] = recv_1[...]

        layer(hid, nrm, ho, wq, wk, wv, wo, seg_c[micro], seg_r[micro], out)


def put_kernel(tick, info, res_0, res_1, kept, buf, done, wide, sem):
    section, micro, active = micro_of(info, tick, 0, ENC)

    @pl.when(active)
    def _():
        table = table_of(kept[micro], ROWS).astype(jnp.bfloat16)
        own = jnp.where(info[1] == 0, res_0[...].astype(jnp.float32), res_1[...].astype(jnp.float32))
        wide[...] = dot(table, own.astype(jnp.bfloat16)).astype(jnp.bfloat16)
        copy = pltpu.make_async_copy(wide, done.at[micro], sem)
        copy.start()
        copy.wait()


def put_wide_kernel(tick, info, res, buf, done, sem):
    section, micro, active = micro_of(info, tick, ENC, SECTIONS)

    @pl.when(active)
    def _():
        copy = pltpu.make_async_copy(res, done.at[micro], sem)
        copy.start()
        copy.wait()


def sign_kernel(sent, res, out, sem):
    copy = pltpu.make_async_copy(sent.at[pl.ds(0, 16), pl.ds(0, 128)], out, sem)
    copy.start()
    copy.wait()


def hold_kernel(rows, token, out):
    pass


def start_kernel(patches, kept, out):
    for micro in range(MICRO):
        table = table_of(kept[micro], ROWS).astype(jnp.bfloat16)
        out[micro] = lax.dot_general(
            table, patches[micro], (((0,), (0,)), ((), ())), preferred_element_type=jnp.float32
        ).astype(jnp.bfloat16)


def cost(rows):
    return pl.CostEstimate(
        flops=2 * 4 * rows * D * D, bytes_accessed=8 * D * D, transcendentals=HEADS * rows * rows
    )


def params():
    return pltpu.CompilerParams(vmem_limit_bytes=6 << 20)


def bf16(*shape):
    return jax.ShapeDtypeStruct(shape, jnp.bfloat16)


def on_device(patches, kept, segment_ids, pos_embed, mask_token, w_query, w_key, w_value, w_out):
    section = lax.axis_index("section")
    core = lax.axis_index("core")
    at_x, at_y = lax.axis_index("x"), lax.axis_index("y")
    info = jnp.stack([section, core, at_x, at_y]).astype(jnp.int32)
    padded = jnp.pad(kept, ((0, 0), (0, KROWS - KEPT)), constant_values=-1)
    hit = padded[:, :, None] == jnp.arange(ROWS, dtype=jnp.int32)[None, None, :]
    kept_seg = jnp.sum(jnp.where(hit, segment_ids[:, None, :], 0), axis=2)
    kept_seg = jnp.where(padded < 0, -1, kept_seg).astype(jnp.int32)
    kept_row = padded[:, None, :]
    enc_c, enc_r = kept_seg[:, :, None], kept_seg[:, None, :]
    dec_c, dec_r = segment_ids[:, :, None], segment_ids[:, None, :]
    mask_row = mask_token[None, :]

    start = pl.pallas_call(
        start_kernel, out_shape=bf16(MICRO, KROWS, D), in_specs=[VM, VM], out_specs=VM,
        compiler_params=params(), name="start_rows",
    )(patches, kept_row)

    weights, decoder_weights = gathered(w_query[0], w_key[0], w_value[0], w_out[0], info)
    weights = [in_vmem(w) for w in weights]

    buf = jnp.zeros((MICRO, ROWS, D), jnp.bfloat16)
    recv_e = jnp.zeros((KROWS, D), jnp.bfloat16)
    recv_d = jnp.zeros((ROWS, D), jnp.bfloat16)
    def encode(tick, recv, only=None, after=info):
        return pl.pallas_call(
            functools.partial(enc_kernel, tick, only), out_shape=bf16(KROWS, D),
            in_specs=[SM] + [VM] * 9 + [HB], out_specs=VM,
            scratch_shapes=[pltpu.VMEM((KROWS, D), jnp.bfloat16)] * 3,
            compiler_params=params(), cost_estimate=cost(KROWS), name="encoder_layer",
        )(info, start, *recv, enc_c, enc_r, *weights, after)

    recv_e, recv_d = (recv_e, recv_e), (recv_d, recv_d)
    for tick in range(MICRO + SECTIONS - 1):
        active = range(max(0, tick - MICRO + 1), min(SECTIONS - 1, tick) + 1)
        next_e, next_d, res_e = recv_e, recv_d, None
        pairs = [(s, s + 1) for s in active if s < ENC]
        if tick == 0:
            both = ("section", "core")
            res_0 = encode(tick, recv_e, only=0)
            sent_0 = lax.ppermute(res_0, both, [(0, 2)])
            token = lax.ppermute(res_0[:16, :128], both, [(0, 1)])
            res_1 = encode(tick, recv_e, only=1, after=token)
            sent_1 = lax.ppermute(res_1, both, [(1, 3)])
            res_e, next_e = (res_0, res_1), (sent_0, sent_1)
        elif active[0] < ENC:
            res = encode(tick, recv_e)
            sent = lax.ppermute(res, "section", pairs)
            res_e, next_e = (res, res), (sent, sent)
        if tick == ENC - 1:
            wide_weights = [in_vmem(w) for w in decoder_weights((recv_e[0][:16],))]
        if active[-1] >= ENC:
            res_d = pl.pallas_call(
                functools.partial(dec_kernel, tick), out_shape=bf16(ROWS, D),
                in_specs=[SM] + [VM] * 12, out_specs=VM,
                scratch_shapes=[pltpu.VMEM((ROWS, D), jnp.bfloat16)] * 3,
                compiler_params=params(), cost_estimate=cost(ROWS), name="decoder_layer",
            )(info, recv_e[0], *recv_d, kept_row, pos_embed, mask_row, dec_c, dec_r, *wide_weights)
            pairs = [(s, s + 1) for s in active if ENC <= s < SECTIONS - 1]
            if tick == ENC:
                both = ("section", "core")
                sent_0 = lax.ppermute(res_d, both, [(2 * ENC, 2 * ENC + 2)])
                sign = pl.pallas_call(
                    sign_kernel, out_shape=bf16(16, 128), in_specs=[HB, HB], out_specs=HB,
                    scratch_shapes=[pltpu.SemaphoreType.DMA], compiler_params=params(),
                    name="sign",
                )(sent_0, next_e[0])
                token = lax.ppermute(sign, both, [(2 * ENC, 2 * ENC + 1)])
                held = pl.pallas_call(
                    hold_kernel, out_shape=bf16(ROWS, D), in_specs=[HB, HB], out_specs=HB,
                    input_output_aliases={0: 0}, compiler_params=params(), name="hold",
                )(res_d, token)
                sent_1 = lax.ppermute(held, both, [(2 * ENC + 1, 2 * ENC + 3)])
                next_d = (sent_0, sent_1)
            elif pairs:
                sent = lax.ppermute(res_d, "section", pairs)
                next_d = (sent, sent)
            buf = pl.pallas_call(
                functools.partial(put_wide_kernel, tick), out_shape=bf16(MICRO, ROWS, D),
                in_specs=[SM, HB, HB], out_specs=HB,
                scratch_shapes=[pltpu.SemaphoreType.DMA],
                input_output_aliases={2: 0}, compiler_params=params(),
                cost_estimate=pl.CostEstimate(
                    flops=0, bytes_accessed=4 * ROWS * D, transcendentals=0
                ),
                name="put_wide",
            )(info, res_d, buf)
        if res_e is not None:
            buf = pl.pallas_call(
                functools.partial(put_kernel, tick), out_shape=bf16(MICRO, ROWS, D),
                in_specs=[SM, VM, VM, VM, HB], out_specs=HB,
                scratch_shapes=[pltpu.VMEM((ROWS, D), jnp.bfloat16), pltpu.SemaphoreType.DMA],
                input_output_aliases={4: 0},
                compiler_params=params(),
                cost_estimate=pl.CostEstimate(
                    flops=2 * ROWS * KROWS * D, bytes_accessed=8 * ROWS * D, transcendentals=0
                ),
                name="put_rows",
            )(info, *res_e, kept_row, buf)
        recv_e, recv_d = next_e, next_d
    return buf[None]


def solution(mesh):
    grid = Mesh(mesh.devices.reshape(SECTIONS, 4, 4, 2), ("section", "x", "y", "core"))
    dp = ("x", "y", "core")
    in_specs = (
        P(dp, None, None),
        P(dp, None),
        P(dp, None),
        P(),
        P(),
        P("section", dp, None),
        P("section", dp, None),
        P("section", dp, None),
        P("section", dp, None),
    )
    out_specs = P("section", dp, None, None)
    return jax.shard_map(
        on_device, mesh=grid, in_specs=in_specs, out_specs=out_specs, check_vma=False
    )
```

```python
import functools
import jax
import jax.numpy as jnp
from jax import lax
from jax.experimental import pallas as pl
from jax.experimental.pallas import tpu as pltpu
from jax.sharding import Mesh, PartitionSpec as P

D = 1536
HEADS = 12
HEAD_DIM = 128
SECTIONS = 8
ENC = 4
MICRO = 3
ROWS = 240
KEPT = 120
KROWS = 128
PART = 48
EPS = 1e-06
LOG2E = 1.4426950408889634
UNROLL = 5
UNROLL_OUT = 6
WSHAPE = (4, 4, 2, PART, D)
VM = pl.BlockSpec(memory_space=pltpu.VMEM)
SM = pl.BlockSpec(memory_space=pltpu.SMEM)
HB = pl.BlockSpec(memory_space=pl.ANY)


def in_vmem(array):
    return pltpu.with_memory_space_constraint(array, pltpu.VMEM)


def move_kernel(count, plan, info, *rest):
    ins, outs = rest[:count], rest[count:]
    for source, at, target, to in plan:
        outs[target][to(info)] = ins[source][...] if at is None else ins[source][at]


def move(info, ins, shapes, plan, name, after=()):
    results = pl.pallas_call(
        lambda info, *refs: move_kernel(len(ins), plan, info, *refs[: len(ins)], *refs[len(ins) + len(after) :]),
        out_shape=[bf16(*shape) for shape in shapes],
        in_specs=[SM] + [VM] * len(ins) + [HB] * len(after),
        out_specs=[VM] * len(shapes),
        compiler_params=pltpu.CompilerParams(vmem_limit_bytes=6 << 20),
        cost_estimate=pl.CostEstimate(flops=0, bytes_accessed=3 << 20, transcendentals=0),
        name=name,
    )(info, *ins, *after)
    return list(results)


def pair_kernel(info, wq, wk, wv, wo, out_0, out_1, sems):
    copies = [
        pltpu.make_async_copy(w, (out_0, out_1)[i % 2].at[i // 2], sems.at[i])
        for i, w in enumerate((wq, wk, wv, wo))
    ]
    for copy in copies:
        copy.start()
    for copy in copies:
        copy.wait()


def pair_up(info, ws):
    ws = [pltpu.with_memory_space_constraint(w, pltpu.HBM) for w in ws]
    return list(
        pl.pallas_call(
            pair_kernel,
            out_shape=[bf16(2, PART, D)] * 2,
            in_specs=[SM] + [HB] * 4,
            out_specs=[HB] * 2,
            scratch_shapes=[pltpu.SemaphoreType.DMA((4,))],
            compiler_params=pltpu.CompilerParams(vmem_limit_bytes=2 << 20),
            name="pair_weights",
        )(info, *ws)
    )


def pack_kernel(count, *rest):
    out, sems = rest[-2:]
    copies = [pltpu.make_async_copy(rest[i], out.at[i], sems.at[i]) for i in range(count)]
    for copy in copies:
        copy.start()
    for copy in copies:
        copy.wait()


def pack(ins, after):
    return pl.pallas_call(
        functools.partial(pack_kernel, len(ins)),
        out_shape=bf16(len(ins), *ins[0].shape),
        in_specs=[HB] * (len(ins) + len(after)),
        out_specs=HB,
        scratch_shapes=[pltpu.SemaphoreType.DMA((len(ins),))],
        compiler_params=pltpu.CompilerParams(vmem_limit_bytes=2 << 20),
        cost_estimate=pl.CostEstimate(flops=0, bytes_accessed=14 << 20, transcendentals=0),
        name="pack",
    )(*ins, *after)


def fixed(*index):
    return lambda info: index


def load_kernel(pieces, first, info, *rest):
    count = len(pieces)
    ins, outs, sems = rest[:count], rest[-5:-1], rest[-1]
    core = info[1]
    todo = []
    for ref, piece in zip(ins, pieces):
        if isinstance(piece, list):
            todo += [(ref.at[i], tag + (True,)) for i, tag in enumerate(piece)]
        else:
            todo.append((ref, piece))
    copies = []
    for ref, (group, shift, half, swapped) in todo:
        side = 1 - core if swapped else core
        far = (info[3 - group] + shift) & 3
        for w in range(2):
            if half is not None and half != w:
                continue
            src = ref if half is not None else ref.at[w]
            at = (slice(None), far, side) if group == 0 else (far, slice(None), side)
            copies.append(
                pltpu.make_async_copy(src, outs[group + 2 * w].at[at], sems.at[len(copies)])
            )

    @pl.when((info[0] >= first) & (info[0] < first + ENC))
    def _():
        for copy in copies:
            copy.start()
        for copy in copies:
            copy.wait()


def load(info, arrays, pieces, first, kept=(), after=()):
    arrays = [pltpu.with_memory_space_constraint(p, pltpu.HBM) for p in arrays]
    kept = [in_vmem(w) for w in kept]
    return pl.pallas_call(
        functools.partial(load_kernel, pieces, first),
        out_shape=[pltpu.VMEM(WSHAPE, jnp.bfloat16)] * 4,
        in_specs=[SM] + [HB] * (len(arrays) + len(after)) + [VM] * len(kept),
        out_specs=[VM] * 4,
        input_output_aliases={1 + len(arrays) + len(after) + i: i for i in range(len(kept))},
        scratch_shapes=[pltpu.SemaphoreType.DMA((32,))],
        compiler_params=pltpu.CompilerParams(vmem_limit_bytes=2 << 20),
        cost_estimate=pl.CostEstimate(flops=0, bytes_accessed=8 * D * D, transcendentals=0),
        name="load_weights",
    )(info, *arrays, *after, *kept)


def shifted(block, axis, by):
    return lax.ppermute(block, axis, [(i, (i + by) % 4) for i in range(4)])


def swapped(block):
    return lax.ppermute(block, "core", [(0, 1), (1, 0)])


def gathered(w_query, w_key, w_value, w_out, info):
    axes = (("x", "y"), ("y", "x"))
    ws = (w_query, w_key, w_value, w_out)
    pairs = pair_up(info, ws)
    near = [[shifted(pairs[g], axes[g][0], by) for by in (1, -1)] for g in range(2)]
    flat = [near[g][i] for g in range(2) for i in range(2)]
    ahead = move(
        info, flat, [(1, PART, D)] * 4, [(i, i % 2, i, fixed(0)) for i in range(4)], "halves"
    )
    across = [
        shifted(ahead[2 * g + i], axes[g][0], (1, -1)[i]) for g in range(2) for i in range(2)
    ]

    def place(group, w, shift):
        return lambda info: (w, (info[2 + group] + shift) & 3)

    plan = []
    for g in range(2):
        for w in range(2):
            plan.append((g, w, g, place(g, w, 0)))
            plan.append((2 + 2 * g, w, g, place(g, w, 3)))
            plan.append((3 + 2 * g, w, g, place(g, w, 1)))
            plan.append((6 + 2 * g + w, 0, g, place(g, w, 2)))
    bands = move(info, pairs + flat + across, [(2, 4, PART, D)] * 2, plan, "bands")
    next_to = [[shifted(bands[g], axes[g][1], by) for by in (1, -1)] for g in range(2)]
    flat = [next_to[g][i] for g in range(2) for i in range(2)]
    ahead = move(
        info, flat, [(1, 4, PART, D)] * 4, [(i, i % 2, i, fixed(0)) for i in range(4)],
        "band_halves",
    )
    last = [
        shifted(ahead[2 * g + i][0], axes[g][1], (1, -1)[i]) for g in range(2) for i in range(2)
    ]
    packed = swapped(pack(bands + flat, ahead))
    tags = [(0, 0, None), (1, 0, None), (0, 3, None), (0, 1, None), (1, 3, None), (1, 1, None)]
    ends = [(g, 2, w) for g in range(2) for w in range(2)]
    early, early_tags = bands + flat + [packed], [t + (False,) for t in tags] + [tags]
    late = last + [swapped(p) for p in last]
    late_tags = [t + (False,) for t in ends] + [t + (True,) for t in ends]
    weights = load(info, early, early_tags, 0)
    weights = load(info, late, late_tags, 0, weights)

    def decoder_weights(after):
        return load(info, early + late, early_tags + late_tags, ENC, after=after)

    return weights, decoder_weights


def rms(x):
    return x * lax.rsqrt(jnp.mean(x * x, axis=-1, keepdims=True) + EPS)


def dot(a, b):
    return jnp.dot(a, b, preferred_element_type=jnp.float32)


def table_of(kept_row, rows):
    pos = lax.broadcasted_iota(jnp.int32, (rows, KROWS), 0)
    return pos == kept_row


def layer(hid, nrm, ho, wq, wk, wv, wo, seg_col, seg_row, out):
    rows = hid.shape[0]
    nrm[...] = rms(hid[...].astype(jnp.float32)).astype(jnp.bfloat16)
    bias = jnp.where(seg_col == seg_row, 0.0, -1e30)
    scale = HEAD_DIM**-0.5 * LOG2E
    ones = jnp.ones((rows, HEAD_DIM), jnp.bfloat16)

    def heads_of(pair):
        cols = pl.ds(pl.multiple_of(pair * 256, 256), 256)

        def project(weight):
            return dot(nrm[...], weight[:, :, :, :, cols].reshape(D, 256))

        q2, k2, v2 = project(wq), project(wk), project(wv).astype(jnp.bfloat16)
        parts = []
        for half in range(2):
            lanes = slice(half * HEAD_DIM, (half + 1) * HEAD_DIM)
            parts.append(rms(q2[:, lanes]).astype(jnp.bfloat16))
            parts.append(rms(k2[:, lanes]).astype(jnp.bfloat16))
            parts.append(v2[:, lanes])
        return tuple(parts)

    def attend(pair, parts):
        cols = pl.ds(pl.multiple_of(pair * 256, 256), 256)
        mixed = []
        for half in range(2):
            q, k, v = parts[3 * half : 3 * half + 3]
            s = lax.dot_general(
                q, k, (((1,), (1,)), ((), ())), preferred_element_type=jnp.float32
            )
            e = jnp.exp2(s * scale + bias).astype(jnp.bfloat16)
            o = dot(e, jnp.concatenate([v, ones], axis=1))
            mixed.append((o[:, :HEAD_DIM] / o[:, HEAD_DIM:]).astype(jnp.bfloat16))
        ho[:, cols] = jnp.concatenate(mixed, axis=1)

    def step(pair, parts):
        later = heads_of(pair + 1)
        attend(pair, parts)
        return later

    last = lax.fori_loop(0, HEADS // 2 - 1, step, heads_of(0), unroll=UNROLL)
    attend(HEADS // 2 - 1, last)

    @pl.loop(0, D // 256, unroll=UNROLL_OUT)
    def _(part):
        cols = pl.ds(pl.multiple_of(part * 256, 256), 256)
        y = dot(ho[...], wo[:, :, :, :, cols].reshape(D, 256))
        out[:, cols] = (hid[:, cols].astype(jnp.float32) + y).astype(jnp.bfloat16)


def micro_of(info, tick, first, last):
    section = info[0]
    micro = tick - section
    active = (micro >= 0) & (micro < MICRO) & (section >= first) & (section < last)
    return section, jnp.clip(micro, 0, MICRO - 1), active


def enc_kernel(
    tick, only, info, start, recv_0, recv_1, seg_c, seg_r, wq, wk, wv, wo, after, out, hid, nrm, ho
):
    section, micro, active = micro_of(info, tick, 0, ENC)
    core = info[1]
    if only is not None:
        active = active & (core == only)

    @pl.when(active)
    def _():
        @pl.when(section == 0)
        def _():
            hid[...] = start[micro]

        @pl.when((section != 0) & (core == 0))
        def _():
            hid[...] = recv_0[...]

        @pl.when((section != 0) & (core == 1))
        def _():
            hid[...] = recv_1[...]

        layer(hid, nrm, ho, wq, wk, wv, wo, seg_c[micro], seg_r[micro], out)


def dec_kernel(
    tick, info, recv_e, recv_0, recv_1, kept, pos, mask, seg_c, seg_r, wq, wk, wv, wo, after, out,
    hid, nrm, ho
):
    section, micro, active = micro_of(info, tick, ENC, SECTIONS)

    @pl.when(active)
    def _():
        @pl.when(section == ENC)
        def _():
            table = table_of(kept[micro], ROWS).astype(jnp.float32)
            flag = jnp.sum(table, axis=1, keepdims=True)
            rows = dot(table.astype(jnp.bfloat16), recv_e[...])
            base = mask[...].astype(jnp.float32) + pos[...].astype(jnp.float32)
            hid[...] = (rows + (1.0 - flag) * base).astype(jnp.bfloat16)

        @pl.when((section != ENC) & (info[1] == 0))
        def _():
            hid[...] = recv_0[...]

        @pl.when((section != ENC) & (info[1] == 1))
        def _():
            hid[...] = recv_1[...]

        layer(hid, nrm, ho, wq, wk, wv, wo, seg_c[micro], seg_r[micro], out)


def put_kernel(tick, info, res_0, res_1, kept, buf, done, wide, sem):
    section, micro, active = micro_of(info, tick, 0, ENC)

    @pl.when(active)
    def _():
        table = table_of(kept[micro], ROWS).astype(jnp.bfloat16)
        own = jnp.where(info[1] == 0, res_0[...].astype(jnp.float32), res_1[...].astype(jnp.float32))
        wide[...] = dot(table, own.astype(jnp.bfloat16)).astype(jnp.bfloat16)
        copy = pltpu.make_async_copy(wide, done.at[micro], sem)
        copy.start()
        copy.wait()


def put_wide_kernel(tick, info, res, buf, done, sem):
    section, micro, active = micro_of(info, tick, ENC, SECTIONS)

    @pl.when(active)
    def _():
        copy = pltpu.make_async_copy(res, done.at[micro], sem)
        copy.start()
        copy.wait()


def sign_kernel(sent, res, out, sem):
    copy = pltpu.make_async_copy(sent.at[pl.ds(0, 16), pl.ds(0, 128)], out, sem)
    copy.start()
    copy.wait()


def hold_kernel(rows, token, out):
    pass


def start_kernel(patches, kept, out):
    for micro in range(MICRO):
        table = table_of(kept[micro], ROWS).astype(jnp.bfloat16)
        out[micro] = lax.dot_general(
            table, patches[micro], (((0,), (0,)), ((), ())), preferred_element_type=jnp.float32
        ).astype(jnp.bfloat16)


def cost(rows):
    return pl.CostEstimate(
        flops=2 * 4 * rows * D * D, bytes_accessed=8 * D * D, transcendentals=HEADS * rows * rows
    )


def params():
    return pltpu.CompilerParams(vmem_limit_bytes=6 << 20)


def bf16(*shape):
    return jax.ShapeDtypeStruct(shape, jnp.bfloat16)


def on_device(patches, kept, segment_ids, pos_embed, mask_token, w_query, w_key, w_value, w_out):
    section = lax.axis_index("section")
    core = lax.axis_index("core")
    at_x, at_y = lax.axis_index("x"), lax.axis_index("y")
    info = jnp.stack([section, core, at_x, at_y]).astype(jnp.int32)
    padded = jnp.pad(kept, ((0, 0), (0, KROWS - KEPT)), constant_values=-1)
    hit = padded[:, :, None] == jnp.arange(ROWS, dtype=jnp.int32)[None, None, :]
    kept_seg = jnp.sum(jnp.where(hit, segment_ids[:, None, :], 0), axis=2)
    kept_seg = jnp.where(padded < 0, -1, kept_seg).astype(jnp.int32)
    kept_row = padded[:, None, :]
    enc_c, enc_r = kept_seg[:, :, None], kept_seg[:, None, :]
    dec_c, dec_r = segment_ids[:, :, None], segment_ids[:, None, :]
    mask_row = mask_token[None, :]

    start = pl.pallas_call(
        start_kernel, out_shape=bf16(MICRO, KROWS, D), in_specs=[VM, VM], out_specs=VM,
        compiler_params=params(), name="start_rows",
    )(patches, kept_row)

    weights, decoder_weights = gathered(w_query[0], w_key[0], w_value[0], w_out[0], info)
    weights = [in_vmem(w) for w in weights]

    buf = jnp.zeros((MICRO, ROWS, D), jnp.bfloat16)
    recv_e = jnp.zeros((KROWS, D), jnp.bfloat16)
    recv_d = jnp.zeros((ROWS, D), jnp.bfloat16)
    def encode(tick, recv, only=None, after=info):
        return pl.pallas_call(
            functools.partial(enc_kernel, tick, only), out_shape=bf16(KROWS, D),
            in_specs=[SM] + [VM] * 9 + [HB], out_specs=VM,
            scratch_shapes=[pltpu.VMEM((KROWS, D), jnp.bfloat16)] * 3,
            compiler_params=params(), cost_estimate=cost(KROWS), name="encoder_layer",
        )(info, start, *recv, enc_c, enc_r, *weights, after)

    recv_e, recv_d = (recv_e, recv_e), (recv_d, recv_d)
    for tick in range(MICRO + SECTIONS - 1):
        active = range(max(0, tick - MICRO + 1), min(SECTIONS - 1, tick) + 1)
        next_e, next_d, res_e = recv_e, recv_d, None
        pairs = [(s, s + 1) for s in active if s < ENC]
        if tick == 0:
            both = ("section", "core")
            res_0 = encode(tick, recv_e, only=0)
            sent_0 = lax.ppermute(res_0, both, [(0, 2)])
            token = lax.ppermute(res_0[:16, :128], both, [(0, 1)])
            res_1 = encode(tick, recv_e, only=1, after=token)
            sent_1 = lax.ppermute(res_1, both, [(1, 3)])
            res_e, next_e = (res_0, res_1), (sent_0, sent_1)
        elif active[0] < ENC:
            res = encode(tick, recv_e)
            sent = lax.ppermute(res, "section", pairs)
            res_e, next_e = (res, res), (sent, sent)
        if tick == ENC - 1:
            wide_weights = [in_vmem(w) for w in decoder_weights((recv_e[0][:16],))]
        if active[-1] >= ENC:
            res_d = pl.pallas_call(
                functools.partial(dec_kernel, tick), out_shape=bf16(ROWS, D),
                in_specs=[SM] + [VM] * 12 + [HB], out_specs=VM,
                scratch_shapes=[pltpu.VMEM((ROWS, D), jnp.bfloat16)] * 3,
                compiler_params=params(), cost_estimate=cost(ROWS), name="decoder_layer",
            )(info, recv_e[0], *recv_d, kept_row, pos_embed, mask_row, dec_c, dec_r, *wide_weights,
              info if res_e is None else res_e[0])
            pairs = [(s, s + 1) for s in active if ENC <= s < SECTIONS - 1]
            if tick == ENC:
                both = ("section", "core")
                sent_0 = lax.ppermute(res_d, both, [(2 * ENC, 2 * ENC + 2)])
                sign = pl.pallas_call(
                    sign_kernel, out_shape=bf16(16, 128), in_specs=[HB, HB], out_specs=HB,
                    scratch_shapes=[pltpu.SemaphoreType.DMA], compiler_params=params(),
                    name="sign",
                )(sent_0, next_e[0])
                token = lax.ppermute(sign, both, [(2 * ENC, 2 * ENC + 1)])
                held = pl.pallas_call(
                    hold_kernel, out_shape=bf16(ROWS, D), in_specs=[HB, HB], out_specs=HB,
                    input_output_aliases={0: 0}, compiler_params=params(), name="hold",
                )(res_d, token)
                sent_1 = lax.ppermute(held, both, [(2 * ENC + 1, 2 * ENC + 3)])
                next_d = (sent_0, sent_1)
            elif pairs:
                sent = lax.ppermute(res_d, "section", pairs)
                next_d = (sent, sent)
            buf = pl.pallas_call(
                functools.partial(put_wide_kernel, tick), out_shape=bf16(MICRO, ROWS, D),
                in_specs=[SM, HB, HB], out_specs=HB,
                scratch_shapes=[pltpu.SemaphoreType.DMA],
                input_output_aliases={2: 0}, compiler_params=params(),
                cost_estimate=pl.CostEstimate(
                    flops=0, bytes_accessed=4 * ROWS * D, transcendentals=0
                ),
                name="put_wide",
            )(info, res_d, buf)
        if res_e is not None:
            buf = pl.pallas_call(
                functools.partial(put_kernel, tick), out_shape=bf16(MICRO, ROWS, D),
                in_specs=[SM, VM, VM, VM, HB], out_specs=HB,
                scratch_shapes=[pltpu.VMEM((ROWS, D), jnp.bfloat16), pltpu.SemaphoreType.DMA],
                input_output_aliases={4: 0},
                compiler_params=params(),
                cost_estimate=pl.CostEstimate(
                    flops=2 * ROWS * KROWS * D, bytes_accessed=8 * ROWS * D, transcendentals=0
                ),
                name="put_rows",
            )(info, *res_e, kept_row, buf)
        recv_e, recv_d = next_e, next_d
    return buf[None]


def solution(mesh):
    grid = Mesh(mesh.devices.reshape(SECTIONS, 4, 4, 2), ("section", "x", "y", "core"))
    dp = ("x", "y", "core")
    in_specs = (
        P(dp, None, None),
        P(dp, None),
        P(dp, None),
        P(),
        P(),
        P("section", dp, None),
        P("section", dp, None),
        P("section", dp, None),
        P("section", dp, None),
    )
    out_specs = P("section", dp, None, None)
    return jax.shard_map(
        on_device, mesh=grid, in_specs=in_specs, out_specs=out_specs, check_vma=False
    )
```

```python
import functools
import jax
import jax.numpy as jnp
from jax import lax
from jax.experimental import pallas as pl
from jax.experimental.pallas import tpu as pltpu
from jax.sharding import Mesh, PartitionSpec as P

D = 1536
HEADS = 12
HEAD_DIM = 128
SECTIONS = 8
ENC = 4
MICRO = 3
ROWS = 240
KEPT = 120
KROWS = 128
PART = 48
EPS = 1e-06
LOG2E = 1.4426950408889634
UNROLL = 5
UNROLL_OUT = 6
WSHAPE = (4, 4, 2, PART, D)
VM = pl.BlockSpec(memory_space=pltpu.VMEM)
SM = pl.BlockSpec(memory_space=pltpu.SMEM)
HB = pl.BlockSpec(memory_space=pl.ANY)


def in_vmem(array):
    return pltpu.with_memory_space_constraint(array, pltpu.VMEM)


def move_kernel(count, plan, info, *rest):
    ins, outs = rest[:count], rest[count:]
    for source, at, target, to in plan:
        outs[target][to(info)] = ins[source][...] if at is None else ins[source][at]


def move(info, ins, shapes, plan, name, after=()):
    results = pl.pallas_call(
        lambda info, *refs: move_kernel(len(ins), plan, info, *refs[: len(ins)], *refs[len(ins) + len(after) :]),
        out_shape=[bf16(*shape) for shape in shapes],
        in_specs=[SM] + [VM] * len(ins) + [HB] * len(after),
        out_specs=[VM] * len(shapes),
        compiler_params=pltpu.CompilerParams(vmem_limit_bytes=6 << 20),
        cost_estimate=pl.CostEstimate(flops=0, bytes_accessed=3 << 20, transcendentals=0),
        name=name,
    )(info, *ins, *after)
    return list(results)


def pair_kernel(info, wq, wk, wv, wo, out_0, out_1, sems):
    copies = [
        pltpu.make_async_copy(w, (out_0, out_1)[i % 2].at[i // 2], sems.at[i])
        for i, w in enumerate((wq, wk, wv, wo))
    ]
    for copy in copies:
        copy.start()
    for copy in copies:
        copy.wait()


def pair_up(info, ws):
    ws = [pltpu.with_memory_space_constraint(w, pltpu.HBM) for w in ws]
    return list(
        pl.pallas_call(
            pair_kernel,
            out_shape=[bf16(2, PART, D)] * 2,
            in_specs=[SM] + [HB] * 4,
            out_specs=[HB] * 2,
            scratch_shapes=[pltpu.SemaphoreType.DMA((4,))],
            compiler_params=pltpu.CompilerParams(vmem_limit_bytes=2 << 20),
            name="pair_weights",
        )(info, *ws)
    )


def pack_kernel(count, *rest):
    out, sems = rest[-2:]
    copies = [pltpu.make_async_copy(rest[i], out.at[i], sems.at[i]) for i in range(count)]
    for copy in copies:
        copy.start()
    for copy in copies:
        copy.wait()


def pack(ins, after):
    return pl.pallas_call(
        functools.partial(pack_kernel, len(ins)),
        out_shape=bf16(len(ins), *ins[0].shape),
        in_specs=[HB] * (len(ins) + len(after)),
        out_specs=HB,
        scratch_shapes=[pltpu.SemaphoreType.DMA((len(ins),))],
        compiler_params=pltpu.CompilerParams(vmem_limit_bytes=2 << 20),
        cost_estimate=pl.CostEstimate(flops=0, bytes_accessed=14 << 20, transcendentals=0),
        name="pack",
    )(*ins, *after)


def fixed(*index):
    return lambda info: index


def load_kernel(pieces, first, info, *rest):
    count = len(pieces)
    ins, outs, sems = rest[:count], rest[-5:-1], rest[-1]
    core = info[1]
    todo = []
    for ref, piece in zip(ins, pieces):
        if isinstance(piece, list):
            todo += [(ref.at[i], tag + (True,)) for i, tag in enumerate(piece)]
        else:
            todo.append((ref, piece))
    copies = []
    for ref, (group, shift, half, swapped) in todo:
        side = 1 - core if swapped else core
        far = (info[3 - group] + shift) & 3
        for w in range(2):
            if half is not None and half != w:
                continue
            src = ref if half is not None else ref.at[w]
            at = (slice(None), far, side) if group == 0 else (far, slice(None), side)
            copies.append(
                pltpu.make_async_copy(src, outs[group + 2 * w].at[at], sems.at[len(copies)])
            )

    @pl.when((info[0] >= first) & (info[0] < first + ENC))
    def _():
        for copy in copies:
            copy.start()
        for copy in copies:
            copy.wait()


def load(info, arrays, pieces, first, kept=(), after=()):
    arrays = [pltpu.with_memory_space_constraint(p, pltpu.HBM) for p in arrays]
    kept = [in_vmem(w) for w in kept]
    return pl.pallas_call(
        functools.partial(load_kernel, pieces, first),
        out_shape=[pltpu.VMEM(WSHAPE, jnp.bfloat16)] * 4,
        in_specs=[SM] + [HB] * (len(arrays) + len(after)) + [VM] * len(kept),
        out_specs=[VM] * 4,
        input_output_aliases={1 + len(arrays) + len(after) + i: i for i in range(len(kept))},
        scratch_shapes=[pltpu.SemaphoreType.DMA((32,))],
        compiler_params=pltpu.CompilerParams(vmem_limit_bytes=2 << 20),
        cost_estimate=pl.CostEstimate(flops=0, bytes_accessed=8 * D * D, transcendentals=0),
        name="load_weights",
    )(info, *arrays, *after, *kept)


def shifted(block, axis, by):
    return lax.ppermute(block, axis, [(i, (i + by) % 4) for i in range(4)])


def swapped(block):
    return lax.ppermute(block, "core", [(0, 1), (1, 0)])


def gathered(w_query, w_key, w_value, w_out, info):
    axes = (("x", "y"), ("y", "x"))
    ws = (w_query, w_key, w_value, w_out)
    pairs = pair_up(info, ws)
    near = [[shifted(pairs[g], axes[g][0], by) for by in (1, -1)] for g in range(2)]
    flat = [near[g][i] for g in range(2) for i in range(2)]
    ahead = move(
        info, flat, [(1, PART, D)] * 4, [(i, i % 2, i, fixed(0)) for i in range(4)], "halves"
    )
    across = [
        shifted(ahead[2 * g + i], axes[g][0], (1, -1)[i]) for g in range(2) for i in range(2)
    ]

    def place(group, w, shift):
        return lambda info: (w, (info[2 + group] + shift) & 3)

    plan = []
    for g in range(2):
        for w in range(2):
            plan.append((g, w, g, place(g, w, 0)))
            plan.append((2 + 2 * g, w, g, place(g, w, 3)))
            plan.append((3 + 2 * g, w, g, place(g, w, 1)))
            plan.append((6 + 2 * g + w, 0, g, place(g, w, 2)))
    bands = move(info, pairs + flat + across, [(2, 4, PART, D)] * 2, plan, "bands")
    next_to = [[shifted(bands[g], axes[g][1], by) for by in (1, -1)] for g in range(2)]
    flat = [next_to[g][i] for g in range(2) for i in range(2)]
    ahead = move(
        info, flat, [(1, 4, PART, D)] * 4, [(i, i % 2, i, fixed(0)) for i in range(4)],
        "band_halves",
    )
    last = [
        shifted(ahead[2 * g + i][0], axes[g][1], (1, -1)[i]) for g in range(2) for i in range(2)
    ]
    packed = swapped(pack(bands + flat, ahead))
    tags = [(0, 0, None), (1, 0, None), (0, 3, None), (0, 1, None), (1, 3, None), (1, 1, None)]
    ends = [(g, 2, w) for g in range(2) for w in range(2)]
    early, early_tags = bands + flat + [packed], [t + (False,) for t in tags] + [tags]
    late = last + [swapped(p) for p in last]
    late_tags = [t + (False,) for t in ends] + [t + (True,) for t in ends]
    weights = load(info, early, early_tags, 0)
    weights = load(info, late, late_tags, 0, weights)

    def decoder_weights(after):
        return load(info, early + late, early_tags + late_tags, ENC, after=after)

    return weights, decoder_weights


def rms(x):
    return x * lax.rsqrt(jnp.mean(x * x, axis=-1, keepdims=True) + EPS)


def dot(a, b):
    return jnp.dot(a, b, preferred_element_type=jnp.float32)


def table_of(kept_row, rows):
    pos = lax.broadcasted_iota(jnp.int32, (rows, KROWS), 0)
    return pos == kept_row


def layer(hid, nrm, ho, wq, wk, wv, wo, seg_col, seg_row, out):
    rows = hid.shape[0]
    nrm[...] = rms(hid[...].astype(jnp.float32)).astype(jnp.bfloat16)
    bias = jnp.where(seg_col == seg_row, 0.0, -1e30)
    scale = HEAD_DIM**-0.5 * LOG2E
    ones = jnp.ones((rows, HEAD_DIM), jnp.bfloat16)

    def heads_of(pair):
        cols = pl.ds(pl.multiple_of(pair * 256, 256), 256)

        def project(weight):
            return dot(nrm[...], weight[:, :, :, :, cols].reshape(D, 256))

        q2, k2, v2 = project(wq), project(wk), project(wv).astype(jnp.bfloat16)
        parts = []
        for half in range(2):
            lanes = slice(half * HEAD_DIM, (half + 1) * HEAD_DIM)
            parts.append(rms(q2[:, lanes]).astype(jnp.bfloat16))
            parts.append(rms(k2[:, lanes]).astype(jnp.bfloat16))
            parts.append(v2[:, lanes])
        return tuple(parts)

    def attend(pair, parts):
        cols = pl.ds(pl.multiple_of(pair * 256, 256), 256)
        mixed = []
        for half in range(2):
            q, k, v = parts[3 * half : 3 * half + 3]
            s = lax.dot_general(
                q, k, (((1,), (1,)), ((), ())), preferred_element_type=jnp.float32
            )
            e = jnp.exp2(s * scale + bias).astype(jnp.bfloat16)
            o = dot(e, jnp.concatenate([v, ones], axis=1))
            mixed.append((o[:, :HEAD_DIM] / o[:, HEAD_DIM:]).astype(jnp.bfloat16))
        ho[:, cols] = jnp.concatenate(mixed, axis=1)

    def step(pair, parts):
        later = heads_of(pair + 1)
        attend(pair, parts)
        return later

    last = lax.fori_loop(0, HEADS // 2 - 1, step, heads_of(0), unroll=UNROLL)
    attend(HEADS // 2 - 1, last)

    @pl.loop(0, D // 256, unroll=UNROLL_OUT)
    def _(part):
        cols = pl.ds(pl.multiple_of(part * 256, 256), 256)
        y = dot(ho[...], wo[:, :, :, :, cols].reshape(D, 256))
        out[:, cols] = (hid[:, cols].astype(jnp.float32) + y).astype(jnp.bfloat16)


def micro_of(info, tick, first, last):
    section = info[0]
    micro = tick - section
    active = (micro >= 0) & (micro < MICRO) & (section >= first) & (section < last)
    return section, jnp.clip(micro, 0, MICRO - 1), active


def enc_kernel(
    tick, only, info, start, recv_0, recv_1, seg_c, seg_r, wq, wk, wv, wo, after, out, hid, nrm, ho
):
    section, micro, active = micro_of(info, tick, 0, ENC)
    core = info[1]
    if only is not None:
        active = active & (core == only)

    @pl.when(active)
    def _():
        if tick < MICRO:

            @pl.when(section == 0)
            def _():
                hid[...] = start[micro]

        if tick == 1:

            @pl.when((section != 0) & (core == 0))
            def _():
                hid[...] = recv_0[...]

            @pl.when((section != 0) & (core == 1))
            def _():
                hid[...] = recv_1[...]

        if tick > 1:

            @pl.when(section != 0)
            def _():
                hid[...] = recv_0[...]

        layer(hid, nrm, ho, wq, wk, wv, wo, seg_c[micro], seg_r[micro], out)


def dec_kernel(
    tick, info, recv_e, recv_0, recv_1, kept, pos, mask, seg_c, seg_r, wq, wk, wv, wo, after, out,
    hid, nrm, ho
):
    section, micro, active = micro_of(info, tick, ENC, SECTIONS)

    @pl.when(active)
    def _():
        if tick < ENC + MICRO:

            @pl.when(section == ENC)
            def _():
                table = table_of(kept[micro], ROWS).astype(jnp.float32)
                flag = jnp.sum(table, axis=1, keepdims=True)
                rows = dot(table.astype(jnp.bfloat16), recv_e[...])
                base = mask[...].astype(jnp.float32) + pos[...].astype(jnp.float32)
                hid[...] = (rows + (1.0 - flag) * base).astype(jnp.bfloat16)

        if tick == ENC + 1:

            @pl.when((section != ENC) & (info[1] == 0))
            def _():
                hid[...] = recv_0[...]

            @pl.when((section != ENC) & (info[1] == 1))
            def _():
                hid[...] = recv_1[...]

        if tick > ENC + 1:

            @pl.when(section != ENC)
            def _():
                hid[...] = recv_0[...]

        layer(hid, nrm, ho, wq, wk, wv, wo, seg_c[micro], seg_r[micro], out)


def put_kernel(tick, info, res_0, res_1, kept, buf, done, wide, sem):
    section, micro, active = micro_of(info, tick, 0, ENC)

    @pl.when(active)
    def _():
        table = table_of(kept[micro], ROWS).astype(jnp.bfloat16)
        own = res_0[...]
        if tick == 0:
            own = jnp.where(info[1] == 0, own.astype(jnp.float32), res_1[...].astype(jnp.float32))
            own = own.astype(jnp.bfloat16)
        wide[...] = dot(table, own).astype(jnp.bfloat16)
        copy = pltpu.make_async_copy(wide, done.at[micro], sem)
        copy.start()
        copy.wait()


def put_wide_kernel(tick, info, res, buf, done, sem):
    section, micro, active = micro_of(info, tick, ENC, SECTIONS)

    @pl.when(active)
    def _():
        copy = pltpu.make_async_copy(res, done.at[micro], sem)
        copy.start()
        copy.wait()


def sign_kernel(sent, res, out, sem):
    copy = pltpu.make_async_copy(sent.at[pl.ds(0, 16), pl.ds(0, 128)], out, sem)
    copy.start()
    copy.wait()


def hold_kernel(rows, token, out):
    pass


def start_kernel(patches, kept, out):
    for micro in range(MICRO):
        table = table_of(kept[micro], ROWS).astype(jnp.bfloat16)
        out[micro] = lax.dot_general(
            table, patches[micro], (((0,), (0,)), ((), ())), preferred_element_type=jnp.float32
        ).astype(jnp.bfloat16)


def cost(rows):
    return pl.CostEstimate(
        flops=2 * 4 * rows * D * D, bytes_accessed=8 * D * D, transcendentals=HEADS * rows * rows
    )


def params():
    return pltpu.CompilerParams(vmem_limit_bytes=6 << 20)


def bf16(*shape):
    return jax.ShapeDtypeStruct(shape, jnp.bfloat16)


def on_device(patches, kept, segment_ids, pos_embed, mask_token, w_query, w_key, w_value, w_out):
    section = lax.axis_index("section")
    core = lax.axis_index("core")
    at_x, at_y = lax.axis_index("x"), lax.axis_index("y")
    info = jnp.stack([section, core, at_x, at_y]).astype(jnp.int32)
    padded = jnp.pad(kept, ((0, 0), (0, KROWS - KEPT)), constant_values=-1)
    hit = padded[:, :, None] == jnp.arange(ROWS, dtype=jnp.int32)[None, None, :]
    kept_seg = jnp.sum(jnp.where(hit, segment_ids[:, None, :], 0), axis=2)
    kept_seg = jnp.where(padded < 0, -1, kept_seg).astype(jnp.int32)
    kept_row = padded[:, None, :]
    enc_c, enc_r = kept_seg[:, :, None], kept_seg[:, None, :]
    dec_c, dec_r = segment_ids[:, :, None], segment_ids[:, None, :]
    mask_row = mask_token[None, :]

    start = pl.pallas_call(
        start_kernel, out_shape=bf16(MICRO, KROWS, D), in_specs=[VM, VM], out_specs=VM,
        compiler_params=params(), name="start_rows",
    )(patches, kept_row)

    weights, decoder_weights = gathered(w_query[0], w_key[0], w_value[0], w_out[0], info)
    weights = [in_vmem(w) for w in weights]

    buf = jnp.zeros((MICRO, ROWS, D), jnp.bfloat16)
    recv_e = jnp.zeros((KROWS, D), jnp.bfloat16)
    recv_d = jnp.zeros((ROWS, D), jnp.bfloat16)
    def encode(tick, recv, only=None, after=info):
        return pl.pallas_call(
            functools.partial(enc_kernel, tick, only), out_shape=bf16(KROWS, D),
            in_specs=[SM] + [VM] * 9 + [HB], out_specs=VM,
            scratch_shapes=[pltpu.VMEM((KROWS, D), jnp.bfloat16)] * 3,
            compiler_params=params(), cost_estimate=cost(KROWS), name="encoder_layer",
        )(info, start, *recv, enc_c, enc_r, *weights, after)

    recv_e, recv_d = (recv_e, recv_e), (recv_d, recv_d)
    for tick in range(MICRO + SECTIONS - 1):
        active = range(max(0, tick - MICRO + 1), min(SECTIONS - 1, tick) + 1)
        next_e, next_d, res_e = recv_e, recv_d, None
        pairs = [(s, s + 1) for s in active if s < ENC]
        if tick == 0:
            both = ("section", "core")
            res_0 = encode(tick, recv_e, only=0)
            sent_0 = lax.ppermute(res_0, both, [(0, 2)])
            token = lax.ppermute(res_0[:16, :128], both, [(0, 1)])
            res_1 = encode(tick, recv_e, only=1, after=token)
            sent_1 = lax.ppermute(res_1, both, [(1, 3)])
            res_e, next_e = (res_0, res_1), (sent_0, sent_1)
        elif active[0] < ENC:
            res = encode(tick, recv_e)
            sent = lax.ppermute(res, "section", pairs)
            res_e, next_e = (res, res), (sent, sent)
        if tick == ENC - 1:
            wide_weights = [in_vmem(w) for w in decoder_weights((recv_e[0][:16],))]
        if active[-1] >= ENC:
            res_d = pl.pallas_call(
                functools.partial(dec_kernel, tick), out_shape=bf16(ROWS, D),
                in_specs=[SM] + [VM] * 12 + [HB], out_specs=VM,
                scratch_shapes=[pltpu.VMEM((ROWS, D), jnp.bfloat16)] * 3,
                compiler_params=params(), cost_estimate=cost(ROWS), name="decoder_layer",
            )(info, recv_e[0], *recv_d, kept_row, pos_embed, mask_row, dec_c, dec_r, *wide_weights,
              info if res_e is None else res_e[0])
            pairs = [(s, s + 1) for s in active if ENC <= s < SECTIONS - 1]
            if tick == ENC:
                both = ("section", "core")
                sent_0 = lax.ppermute(res_d, both, [(2 * ENC, 2 * ENC + 2)])
                sign = pl.pallas_call(
                    sign_kernel, out_shape=bf16(16, 128), in_specs=[HB, HB], out_specs=HB,
                    scratch_shapes=[pltpu.SemaphoreType.DMA], compiler_params=params(),
                    name="sign",
                )(sent_0, next_e[0])
                token = lax.ppermute(sign, both, [(2 * ENC, 2 * ENC + 1)])
                held = pl.pallas_call(
                    hold_kernel, out_shape=bf16(ROWS, D), in_specs=[HB, HB], out_specs=HB,
                    input_output_aliases={0: 0}, compiler_params=params(), name="hold",
                )(res_d, token)
                sent_1 = lax.ppermute(held, both, [(2 * ENC + 1, 2 * ENC + 3)])
                next_d = (sent_0, sent_1)
            elif pairs:
                sent = lax.ppermute(res_d, "section", pairs)
                next_d = (sent, sent)
            buf = pl.pallas_call(
                functools.partial(put_wide_kernel, tick), out_shape=bf16(MICRO, ROWS, D),
                in_specs=[SM, HB, HB], out_specs=HB,
                scratch_shapes=[pltpu.SemaphoreType.DMA],
                input_output_aliases={2: 0}, compiler_params=params(),
                cost_estimate=pl.CostEstimate(
                    flops=0, bytes_accessed=4 * ROWS * D, transcendentals=0
                ),
                name="put_wide",
            )(info, res_d, buf)
        if res_e is not None:
            buf = pl.pallas_call(
                functools.partial(put_kernel, tick), out_shape=bf16(MICRO, ROWS, D),
                in_specs=[SM, VM, VM, VM, HB], out_specs=HB,
                scratch_shapes=[pltpu.VMEM((ROWS, D), jnp.bfloat16), pltpu.SemaphoreType.DMA],
                input_output_aliases={4: 0},
                compiler_params=params(),
                cost_estimate=pl.CostEstimate(
                    flops=2 * ROWS * KROWS * D, bytes_accessed=8 * ROWS * D, transcendentals=0
                ),
                name="put_rows",
            )(info, *res_e, kept_row, buf)
        recv_e, recv_d = next_e, next_d
    return buf[None]


def solution(mesh):
    grid = Mesh(mesh.devices.reshape(SECTIONS, 4, 4, 2), ("section", "x", "y", "core"))
    dp = ("x", "y", "core")
    in_specs = (
        P(dp, None, None),
        P(dp, None),
        P(dp, None),
        P(),
        P(),
        P("section", dp, None),
        P("section", dp, None),
        P("section", dp, None),
        P("section", dp, None),
    )
    out_specs = P("section", dp, None, None)
    return jax.shard_map(
        on_device, mesh=grid, in_specs=in_specs, out_specs=out_specs, check_vma=False
    )
```
